128 devices in a mesh: airway: 8 (over y, core), section: 16 (over z, x).
Axes of the slice: x: 4, y: 4, z: 4, core: 2. Of those that a mesh axis runs over, the one named last changes fastest.
Arguments:
- fluid_velocity: float32 [3, 64, 128, 2048], P(None, None, 'section', 'airway'), may hold values from -6 to 6
- viscosity: float32 [128, 2048], P('section', 'airway'), may hold values from 0.002 to 0.008
- axial_speed: float32 [128, 2048], P('section', 'airway'), may hold values from 0.01 to 0.04
- fluid_mass: float32 [128, 2048], P('section', 'airway'), may hold values from 2 to 8
- positions: float32 [24576, 3, 128], P(('airway', 'section')), may hold values from -1 to 1
- velocities: float32 [24576, 3, 128], P(('airway', 'section')), may hold values from -6 to 6
- relax_rates: float32 [24576, 128], P(('airway', 'section')), may hold values from 0.02 to 0.5
- bin_element: int32 [24576], P(('airway', 'section')), may hold values from 0 to 2047
- bin_fill: int32 [24576], P(('airway', 'section')), may hold values from 0 to 128, as said below
Outputs:
- fluid_out: float32 [3, 64, 128, 2048], P(None, None, 'section', 'airway')
- particles_out: float32 [24576, 6, 128], P(('airway', 'section'))
The draws below stay inside these ranges and needn't reach their ends.
Inputs may be any that keep to these rules, and one draw needn't show every extreme that they name: `bin_fill`: on each device the bins with particles are the first 64 + k slots, k from 0 to 128; over all devices the k sum to exactly 8192, and k = 128 on some device. Every device's first slot holds 128 particles.
All inputs are finite; a program needn't handle non-finite values.
Results may differ from the reference program's by a relative error of at most 0.00023.
Values sent between devices are 32-bit elements; how exact they have to be, the bound alone decides.
A program may use at most 64 MiB of HBM per device.

```python
import math
import jax
import jax.numpy as jnp
import numpy as np
from jax import lax

NODES = 64
PER_BIN = 128
SUBSTEPS = 16
PASSES = 4
EA_DEV = 256
ES_DEV = 8
HOME = 64
EA = 2048
ES = 128
OVER = 128
BINS_CAP = 192
NB = 24576
N_SECTION = 16


def draw_bin_fill(key, part):
    key_order = jax.random.fold_in(key, 101)
    key_shares = jax.random.fold_in(key, 202)
    key_counts = jax.random.fold_in(key, 303)
    device_order = jax.random.permutation(key_order, OVER)
    shares = jax.random.randint(key_shares, (OVER // 2,), 0, OVER + 1)
    shares = shares.at[0].set(OVER)
    overflow = jnp.zeros((OVER,), jnp.int32)
    overflow = overflow.at[device_order[0::2]].set(shares)
    overflow = overflow.at[device_order[1::2]].set(OVER - shares)
    occupied_slots = HOME + overflow
    slot_index = jnp.arange(BINS_CAP, dtype=jnp.int32)
    fill_counts = jax.random.randint(key_counts, (OVER, BINS_CAP), 1, PER_BIN + 1)
    fill_counts = fill_counts.at[:, 0].set(PER_BIN)
    result = jnp.where(slot_index[None, :] < occupied_slots[:, None], fill_counts, 0)
    return result.reshape(-1).astype(jnp.int32)


def set_ends(values, rng, smallest, high):
    spot = [jax.random.randint(jax.random.fold_in(rng, axis), (), 0, length) for axis, length in enumerate(values.shape)]
    main_axis = values.shape.index(max(values.shape))
    neighbour = spot[:main_axis] + [(spot[main_axis] + 1) % values.shape[main_axis]] + spot[main_axis + 1:]
    return values.at[tuple(spot)].set(smallest).at[tuple(neighbour)].set(high)


def block_scale(key, shape, cuts, smallest, largest):
    def one(dim, shards_of):
        steps = jax.random.uniform(jax.random.fold_in(jax.random.fold_in(key, 6), dim), (shards_of,), jnp.float32, smallest / len(cuts), largest / len(cuts))
        return jnp.repeat(jnp.exp(steps), shape[dim] // shards_of).reshape((-1,) + (1,) * (len(shape) - dim - 1))

    factor_of = one(*cuts[0])
    for cut in cuts[1:]:
        factor_of = factor_of * one(*cut)
    return factor_of


def noise(own_key, extent, deviation, bound, shards=(), kind=jnp.bfloat16):
    values = jax.random.normal(own_key, extent, jnp.float32) * deviation
    if len(shards) > 0:
        values = block_scale(own_key, extent, shards, -0.22, 0.18) * values
    return jnp.clip(values, min=-bound, max=bound).astype(kind)


def setup_inputs(seed: int = 0) -> dict:
    arg_keys = jax.random.split(jax.random.key(seed), 10)
    fluid_velocity = noise(arg_keys[0], (3, NODES, ES, EA), 1.0, 6.0, ((2, 16), (3, 8)), jnp.float32)
    viscosity = jnp.clip(jnp.exp(math.log(0.008) - 1.3862944 * jax.random.uniform(arg_keys[1], (ES, EA), jnp.float32) ** block_scale(arg_keys[1], (ES, EA), ((0, 16), (1, 8)), -0.2, 0.2)), 0.002, 0.008)
    axial_speed = jnp.clip(0.01 + 0.03 * jax.random.uniform(arg_keys[2], (ES, EA), jnp.float32) ** block_scale(arg_keys[2], (ES, EA), ((0, 16), (1, 8)), -0.2, 0.2), 0.01, 0.04)
    fluid_mass = jnp.clip(jnp.exp(math.log(8.0) - 1.3862944 * jax.random.uniform(arg_keys[3], (ES, EA), jnp.float32) ** block_scale(arg_keys[3], (ES, EA), ((0, 16), (1, 8)), -0.2, 0.2)), 2.0, 8.0)
    positions = jnp.clip(jax.random.uniform(arg_keys[4], (NB, 3, PER_BIN), jnp.float32, -1.0, 1.0) * block_scale(arg_keys[4], (NB, 3, PER_BIN), ((0, 128),), -0.4, 0.0), -1.0, 1.0)
    velocities = noise(arg_keys[5], (NB, 3, PER_BIN), 1.0, 6.0, ((0, 128),), jnp.float32)
    relax_rates = jnp.clip(jnp.exp(math.log(0.5) - 3.218876 * jax.random.uniform(arg_keys[6], (NB, PER_BIN), jnp.float32) ** block_scale(arg_keys[6], (NB, PER_BIN), ((0, 128),), -0.2, 0.2)), 0.02, 0.5)
    bin_element = set_ends(jax.random.randint(arg_keys[7], (NB,), 0, ES_DEV * EA_DEV), jax.random.fold_in(arg_keys[7], 1), 0, (ES_DEV * EA_DEV) - 1).astype(jnp.int32)
    bin_fill = draw_bin_fill(jax.random.fold_in(arg_keys[9], 71), 0)
    return {"fluid_velocity": fluid_velocity, "viscosity": viscosity, "axial_speed": axial_speed, "fluid_mass": fluid_mass, "positions": positions, "velocities": velocities, "relax_rates": relax_rates, "bin_element": bin_element, "bin_fill": bin_fill}


node_coords = (-1.0, -1.0 / 3.0, 1.0 / 3.0, 1.0)
penalty_weight = 0.25
stride_step = 0.05
exact_mode = lax.Precision.HIGHEST


def deriv_table():
    matrix = np.zeros((4, 4))
    for row_node in range(4):
        for col_node in range(4):
            summed = 0.0
            for skip_node in range(4):
                if skip_node != col_node:
                    factor = 1.0 / (node_coords[col_node] - node_coords[skip_node])
                    for third_node in range(4):
                        if third_node != col_node and third_node != skip_node:
                            factor = factor * (node_coords[row_node] - node_coords[third_node]) / (node_coords[col_node] - node_coords[third_node])
                    summed = summed + factor
            matrix[row_node, col_node] = summed
    return matrix


def operator_table():
    first_deriv = deriv_table()
    second_deriv = first_deriv @ first_deriv
    identity = np.eye(4)
    laplace = np.kron(np.kron(second_deriv, identity), identity) + np.kron(np.kron(identity, second_deriv), identity) + np.kron(np.kron(identity, identity), second_deriv)
    airway_grad = np.kron(np.kron(first_deriv, identity), identity)
    return np.concatenate([laplace, airway_grad], axis=0).astype(np.float32)


def basis_values(coordinate):
    values = []
    for centre in range(4):
        factor = jnp.ones_like(coordinate)
        for second in range(4):
            if second != centre:
                factor = factor * (coordinate - node_coords[second]) / (node_coords[centre] - node_coords[second])
        values.append(factor)
    return jnp.stack(values, axis=1)


def drag_bins(records, nodal_velocity):
    batch_size = records.shape[0]
    fluid_nodes = nodal_velocity.reshape(batch_size, 3, NODES)
    relax_rate = records[:, 6]
    occupied = records[:, 7]

    def substep(turn_index, carried):
        position, velocity, drag_sum, weight_sum = carried
        basis_one = basis_values(position[:, 0])
        basis_two = basis_values(position[:, 1])
        basis_three = basis_values(position[:, 2])
        weights = (basis_one[:, :, None, None, :] * basis_two[:, None, :, None, :] * basis_three[:, None, None, :, :]).reshape(batch_size, NODES, -1)
        at_particle = jnp.einsum("bcn,bnp->bcp", fluid_nodes, weights, precision=exact_mode)
        change = (relax_rate * occupied)[:, None, :] * (at_particle - velocity)
        velocity = velocity + change
        position = jnp.clip(position + stride_step * occupied[:, None, :] * velocity, -1.0, 1.0)
        drag_sum = drag_sum + jnp.einsum("bnp,bcp->bcn", weights, change, precision=exact_mode)
        weight_sum = weight_sum + jnp.einsum("bnp,bp->bn", weights * weights, occupied, precision=exact_mode)
        return position, velocity, drag_sum, weight_sum

    start_state = (records[:, 0:3], records[:, 3:6], jnp.zeros((batch_size, 3, NODES), jnp.float32), jnp.zeros((batch_size, NODES), jnp.float32))
    position, velocity, drag_sum, weight_sum = lax.fori_loop(0, SUBSTEPS, substep, start_state)
    moved_state = jnp.concatenate([position, velocity], axis=1)
    nodal_sums = jnp.concatenate([drag_sum.reshape(batch_size, 3 * NODES), weight_sum], axis=1)
    return moved_state, nodal_sums


def local_update(field, viscosity, axial_speed, after_airway, before_airway, after_section, before_section):
    operator = jnp.asarray(operator_table(), dtype=jnp.float32)
    applied = jnp.einsum("mn,cnse->cmse", operator, field, precision=exact_mode)
    cube = field.reshape((3, 4, 4, 4) + field.shape[2:])
    faces = jnp.zeros_like(cube)
    faces = faces.at[:, 3].add(after_airway - cube[:, 3])
    faces = faces.at[:, 0].add(before_airway - cube[:, 0])
    faces = faces.at[:, :, 3].add(after_section - cube[:, :, 3])
    faces = faces.at[:, :, 0].add(before_section - cube[:, :, 0])
    return field + viscosity * applied[:, :NODES] - axial_speed * applied[:, NODES:] + penalty_weight * faces.reshape(field.shape)


def reference(fluid_velocity, viscosity, axial_speed, fluid_mass, positions, velocities, relax_rates, bin_element, bin_fill):
    occupancy = (jnp.arange(PER_BIN, dtype=jnp.int32)[None, :] < bin_fill[:, None]).astype(jnp.float32)
    records = jnp.concatenate([positions, velocities, relax_rates[:, None, :], occupancy[:, None, :]], axis=1)
    device_rank = jnp.arange(NB, dtype=jnp.int32) // BINS_CAP
    air_block = device_rank // N_SECTION
    sec_block = device_rank % N_SECTION
    global_element = ((sec_block * ES_DEV + bin_element // EA_DEV) * EA + air_block * EA_DEV + bin_element % EA_DEV).astype(jnp.int32)
    flat_fluid = fluid_velocity.reshape(3 * NODES, ES * EA)

    def one_block(pieces):
        block_records, block_element = pieces
        block_nodal = jnp.take(flat_fluid, block_element, axis=1).T
        return drag_bins(block_records, block_nodal)

    moved_state, nodal_sums = lax.map(one_block, (records.reshape(OVER, BINS_CAP, 8, PER_BIN), global_element.reshape(OVER, BINS_CAP)))
    particles_out = moved_state.reshape(NB, 6, PER_BIN)
    deposited = jax.ops.segment_sum(nodal_sums.reshape(NB, 4 * NODES), global_element, num_segments=ES * EA).T
    drag_part = deposited[:3 * NODES].reshape(3, NODES, ES, EA)
    weight_part = deposited[3 * NODES:].reshape(NODES, ES, EA)
    field = fluid_velocity - drag_part / (fluid_mass[None, None] + weight_part[None])
    for pass_index in range(PASSES):
        cube = field.reshape(3, 4, 4, 4, ES, EA)
        padded = jnp.pad(cube, ((0, 0), (0, 0), (0, 0), (0, 0), (1, 1), (1, 1)))
        field = local_update(field, viscosity, axial_speed, padded[:, 0, :, :, 1:-1, 2:], padded[:, 3, :, :, 1:-1, :-2], padded[:, :, 0, :, 2:, 1:-1], padded[:, :, 3, :, :-2, 1:-1])
    return field, particles_out
```

```python
import functools
import jax, jax.numpy as jnp, numpy as np
from jax import lax
from jax.experimental import pallas as pl
from jax.experimental.pallas import tpu as pltpu

F32, BF16 = jnp.float32, jnp.bfloat16
BINS, GROUPS, SUB, SUBSTEPS = 192, 24, 8, 16
NT = (((1,), (1,)), ((), ()))
TN = (((0,), (0,)), ((), ()))

def dot(a, b, dims=(((1,), (0,)), ((), ()))):
    return lax.dot_general(a, b, dims, preferred_element_type=F32)

def split(x):
    hi = x.astype(BF16)
    return hi, (x - hi.astype(F32)).astype(BF16)

def basis(x):
    s = x * x
    outer = s * (9 / 16) - (1 / 16)
    inner = s * (27 / 16) - (27 / 16)
    return [outer - outer * x, inner * (x - 1 / 3), -(inner * (x + 1 / 3)), outer + outer * x]

def pairs(tiles):
    return [jnp.concatenate(tiles[i:i + 2], axis=0) for i in range(0, len(tiles), 2)]

def split_tiles(tiles):
    both = [split(p) for p in pairs(tiles)]
    return jnp.concatenate([b[0] for b in both], axis=0), jnp.concatenate([b[1] for b in both], axis=0)

def ioeq(shape, f):
    r = lax.broadcasted_iota(jnp.int32, shape, 0)
    c = lax.broadcasted_iota(jnp.int32, shape, 1)
    return jnp.where(f(r, c), 1.0, 0.0)

def drag_kernel(unroll, elem_col, elem_row, fill, fluid, mass, pos, vel, relax, coupled, pout, nodal, state, acc, dep):
    hi = jnp.zeros((BINS, BINS), F32)
    lo = jnp.zeros((BINS, BINS), F32)
    cols = lax.broadcasted_iota(jnp.int32, (BINS, 256), 1)
    for r in range(8):
        fh, fl = split(fluid[:, r, :])
        oh = jnp.where(elem_col[...] == cols + r * 256, 1.0, 0.0).astype(BF16)
        hi += dot(oh, fh, NT)
        lo += dot(oh, fl, NT)
    hi, lo = hi.astype(BF16), lo.astype(BF16)
    diag = ioeq((BINS, 128), lambda r, c: r % 8 == c % 8)
    for cp in range(6):
        for k, piece in enumerate((hi, lo)):
            both = []
            for ca in (2 * cp, 2 * cp + 1):
                rep = ioeq((BINS, 128), lambda r, c: r == ca * 16 + c // 8).astype(BF16)
                both.append((dot(piece, rep) * diag).reshape(GROUPS, 8, 128))
            both = jnp.concatenate(both, axis=1).astype(BF16)
            if k == 0:
                nodal[:, cp * 16:cp * 16 + 16, 0:128] = both
                nodal[:, cp * 16:cp * 16 + 16, 128:256] = both
            else:
                nodal[:, cp * 16:cp * 16 + 16, 256:384] = both
    occ = jnp.where(lax.broadcasted_iota(jnp.int32, (BINS, 128), 1) < fill[...], 1.0, 0.0)
    state[0:3] = pos[...]
    state[3:6] = vel[...]
    state[6] = relax[...] * occ
    state[7] = occ
    acc[...] = jnp.zeros_like(acc)

    def first(g):
        rows = pl.ds(pl.multiple_of(g * 8, 8), 8)
        x = [state[i, rows, :] for i in range(3)]
        l0, l1, l2 = (basis(t) for t in x)
        lh, ll = split_tiles([b * c for b in l1 for c in l2])
        return g, rows, x, l0, lh, ll, dot(nodal[g], jnp.concatenate([lh, ll, lh], axis=0))

    def second(args):
        g, rows, x, l0, lh, ll, both = args
        v = [state[3 + i, rows, :] for i in range(3)]
        ro, oc = state[6, rows, :], state[7, rows, :]
        stride = oc * 0.05
        forces = []
        for c in range(3):
            t = [l0[a] * both[(4 * c + a) * 8:(4 * c + a) * 8 + 8] for a in range(4)]
            u = (t[0] + t[1]) + (t[2] + t[3])
            dv = ro * (u - v[c])
            nv = v[c] + dv
            state[3 + c, rows, :] = nv
            state[c, rows, :] = jnp.clip(x[c] + stride * nv, -1.0, 1.0)
            forces += [dv * l0[a] for a in range(4)]
        fh, fl = split_tiles(forces)
        wa = jnp.concatenate([p.astype(BF16) for p in pairs([oc * (l * l) for l in l0])], axis=0)
        lt = lh.T
        drag = dot(jnp.concatenate([fh, fl, fh], axis=1), jnp.concatenate([lt, lt, ll.T], axis=0))
        return g, drag, dot(wa, lt * lt)

    def third(args):
        g, drag, weight = args
        acc[g, 0:96] += drag
        acc[g, 96:128] += weight

    def substep(t, _):
        def block(k, _):
            mid = [first(k * unroll + j) for j in range(unroll)]
            end = [second(m) for m in mid]
            for e in end: third(e)
            return 0
        lax.fori_loop(0, GROUPS // unroll, block, 0)
        return 0
    lax.fori_loop(0, SUBSTEPS, substep, 0)
    pout[...] = state[0:6]
    sums = jnp.zeros((BINS, 256), F32)
    for ca in range(16):
        a = acc[:, ca * 8:ca * 8 + 8, :].reshape(BINS, 128) * diag
        ah, al = split(a)
        rep = ioeq((256, 128), lambda r, c: r == ca * 16 + c // 8).astype(BF16)
        sums += dot(ah, rep, NT) + dot(al, rep, NT)
    sh, sl = split(sums.T)
    stacked = jnp.concatenate([sh, sl], axis=1)
    for r in range(8):
        oh = jnp.where(elem_col[...] == cols + r * 256, 1.0, 0.0).astype(BF16)
        dep[:, r, :] = dot(stacked, jnp.concatenate([oh, oh], axis=0))
    inv = 1.0 / (mass[...][None] + dep[192:256])
    for c in range(3):
        s = slice(c * 64, c * 64 + 64)
        coupled[s] = fluid[s] - dep[s] * inv

def drag(fluid, mass, pos, vel, relax, elem, fill, unroll=2):
    return pl.pallas_call(
        functools.partial(drag_kernel, unroll),
        out_shape=(jax.ShapeDtypeStruct((192, 8, 256), F32), jax.ShapeDtypeStruct((6, BINS, 128), F32)),
        scratch_shapes=[pltpu.VMEM((GROUPS, 96, 384), BF16), pltpu.VMEM((8, BINS, 128), F32),
                        pltpu.VMEM((GROUPS, 128, 128), F32), pltpu.VMEM((256, 8, 256), F32)],
        compiler_params=pltpu.CompilerParams(vmem_limit_bytes=56 * 2**20),
    )(elem.reshape(BINS, 1), elem.reshape(1, BINS), fill.reshape(BINS, 1), fluid, mass, pos, vel, relax)


PASSES = 4
MESH = pl.DeviceIdType.MESH


def curvature(line):
    low = line[0] - 2.0 * line[1] + line[2]
    high = line[1] - 2.0 * line[2] + line[3]
    step = low - high
    return [low + step, low, high, high - step]


CURVE = ((-2, 3, -1), (-1, 1, 0), (0, -1, 1), (1, -3, 2))
SLOPE = ((11, -7, 2), (2, 5, -1), (-1, 5, 2), (2, -7, 11))


def section_phase(src, dst, visc, sub):
    up = jnp.where(sub == 7, 0.0, 0.25)
    down = jnp.where(sub == 0, 0.0, 0.25)

    def body(i, _):
        base = pl.multiple_of(i * 16, 16)
        t = [[src[base + 4 * b + c] for c in range(4)] for b in range(4)]
        across = [curvature([t[b][c] for b in range(4)]) for c in range(4)]
        for b in range(4):
            along = curvature(t[b])
            for c in range(4):
                new = t[b][c] + visc * (along[c] + across[c][b])
                if b == 3:
                    new = new - 0.25 * t[3][c] + up * pltpu.roll(t[0][c], 7, 0)
                if b == 0:
                    new = new - 0.25 * t[0][c] + down * pltpu.roll(t[3][c], 1, 0)
                dst[base + 4 * b + c] = new
        return 0

    lax.fori_loop(0, 12, body, 0)


def airway_phase(src, dst, mix, lane):
    fore = jnp.where(lane == 255, 0.0, 0.25)
    back = jnp.where(lane == 0, 0.0, 0.25)

    def body(i, _):
        base = (i // 4) * 64 + (i % 4) * 4
        for c in range(4):
            at = [base + 16 * a + c for a in range(4)]
            q = [src[n] for n in at]
            d = [q[k + 1] - q[k] for k in range(3)]
            for a in range(4):
                new = dst[at[a]] + mix[3 * a] * d[0] + mix[3 * a + 1] * d[1] + mix[3 * a + 2] * d[2]
                if a == 3:
                    new = new - 0.25 * q[3] + fore * pltpu.roll(q[0], 255, 1)
                if a == 0:
                    new = new - 0.25 * q[0] + back * pltpu.roll(q[3], 1, 1)
                dst[at[a]] = new
        return 0

    lax.fori_loop(0, 12, body, 0)


def air_nodes(a):
    return [comp * 64 + a * 16 + k for comp in range(3) for k in range(16)]


def sec_nodes(b):
    return [comp * 64 + a * 16 + b * 4 + c for comp in range(3) for a in range(4) for c in range(4)]


def fluid_kernel(field, viscosity, speed, out, ping, pong, mix, s_sec, s_air, r_sec, r_air, send_sem, recv_sem):
    me_a, me_s = lax.axis_index("airway"), lax.axis_index("section")
    n_a, n_s = lax.axis_size("airway"), lax.axis_size("section")
    peers = [(me_a, lax.rem(me_s + 1, n_s)), (me_a, lax.rem(me_s + n_s - 1, n_s)),
             (lax.rem(me_a + 1, n_a), me_s), (lax.rem(me_a + n_a - 1, n_a), me_s)]
    barrier = pltpu.get_barrier_semaphore()
    for p in peers:
        pl.semaphore_signal(barrier, inc=1, device_id=p, device_id_type=MESH)
    visc = viscosity[...] * 2.25
    quarter = speed[...] * 0.25
    for a in range(4):
        for k in range(3):
            mix[3 * a + k] = CURVE[a][k] * visc - SLOPE[a][k] * quarter
    sub = lax.broadcasted_iota(jnp.int32, (8, 256), 0)
    lane = lax.broadcasted_iota(jnp.int32, (8, 256), 1)
    lane1 = lax.broadcasted_iota(jnp.int32, (8, 128), 1)
    some = lambda cond: jnp.where(cond, 0.25, 0.0).astype(F32)
    next_s, prev_s = some(me_s < n_s - 1), some(me_s > 0)
    next_a, prev_a = some(me_a < n_a - 1), some(me_a > 0)
    pl.semaphore_wait(barrier, 4)
    bufs = [field, ping, pong, ping, out]
    for p in range(PASSES):
        src, dst = bufs[p], bufs[p + 1]
        for slot, row, b in ((0, 7, 3), (1, 0, 0)):
            for j, n in enumerate(sec_nodes(b)):
                s_sec[p, slot, j:j + 1, :] = src[n, row:row + 1, :]
        for slot, base, a in ((0, 128, 3), (1, 0, 0)):
            packed = jnp.zeros((8, 128), F32)
            col = 127 if slot == 0 else 0
            for j, n in enumerate(air_nodes(a)):
                moved = pltpu.roll(src[n, :, base:base + 128], (j - col) % 128, 1)
                packed = jnp.where(lane1 == j, moved, packed)
            s_air[p, slot] = packed
        copies = []
        for k in range(4):
            s, r = (s_sec, r_sec) if k < 2 else (s_air, r_air)
            copies.append(pltpu.make_async_remote_copy(
                src_ref=s.at[p, k % 2], dst_ref=r.at[p, k % 2], send_sem=send_sem.at[p, k], recv_sem=recv_sem.at[p, k],
                device_id=peers[k], device_id_type=MESH))
            copies[-1].start()
        section_phase(src, dst, visc, sub)
        airway_phase(src, dst, mix, lane)
        for c in copies:
            c.wait()
        for slot, row, b, scale in ((0, 0, 0, prev_s), (1, 7, 3, next_s)):
            for j, n in enumerate(sec_nodes(b)):
                dst[n, row:row + 1, :] += scale * r_sec[p, slot, j:j + 1, :]
        for slot, base, a, scale in ((0, 0, 0, prev_a), (1, 128, 3, next_a)):
            col = 0 if slot == 0 else 127
            packed = r_air[p, slot] * scale
            for j, n in enumerate(air_nodes(a)):
                moved = pltpu.roll(packed, (col - j) % 128, 1)
                dst[n, :, base:base + 128] += jnp.where(lane1 == col, moved, 0.0)


def advance(field, viscosity, speed):
    vm = pl.BlockSpec(memory_space=pltpu.VMEM)
    return pl.pallas_call(
        fluid_kernel,
        out_shape=jax.ShapeDtypeStruct((192, 8, 256), F32),
        in_specs=[vm] * 3,
        out_specs=vm,
        scratch_shapes=[pltpu.VMEM((192, 8, 256), F32), pltpu.VMEM((192, 8, 256), F32), pltpu.VMEM((12, 8, 256), F32),
                        pltpu.VMEM((PASSES, 2, 48, 256), F32), pltpu.VMEM((PASSES, 2, 8, 128), F32),
                        pltpu.VMEM((PASSES, 2, 48, 256), F32), pltpu.VMEM((PASSES, 2, 8, 128), F32),
                        pltpu.SemaphoreType.DMA((PASSES, 4)), pltpu.SemaphoreType.DMA((PASSES, 4))],
        compiler_params=pltpu.CompilerParams(collective_id=0, has_side_effects=True, vmem_limit_bytes=56 * 2**20),
    )(field, viscosity, speed)

def local(fluid_velocity, viscosity, axial_speed, fluid_mass, positions, velocities, relax_rates, bin_element, bin_fill):
    field = fluid_velocity.reshape(192, 8, 256)
    coupled, moved = drag(field, fluid_mass, positions.transpose(1, 0, 2), velocities.transpose(1, 0, 2), relax_rates,
                          bin_element, bin_fill, 8)
    return advance(coupled, viscosity, axial_speed).reshape(fluid_velocity.shape), moved.transpose(1, 0, 2)


def solution(mesh):
    from jax.sharding import PartitionSpec as P
    bins = ("airway", "section")
    cells = P("section", "airway")
    return jax.shard_map(
        local,
        mesh=mesh,
        in_specs=(P(None, None, *cells), cells, cells, cells, P(bins, None, None), P(bins, None, None), P(bins, None),
                  P(bins), P(bins)),
        out_specs=(P(None, None, *cells), P(bins, None, None)),
        check_vma=False,
    )
```

```python
import functools
import jax, jax.numpy as jnp, numpy as np
from jax import lax
from jax.experimental import pallas as pl
from jax.experimental.pallas import tpu as pltpu
from jax.sharding import PartitionSpec as P

F32, BF16 = jnp.float32, jnp.bfloat16
BINS, GROUPS, SUBSTEPS = 192, 24, 16
cat = jnp.concatenate


def dot(a, b):
    return jnp.dot(a, b, preferred_element_type=F32)


def split(x):
    hi = x.astype(BF16)
    return hi, (x - hi.astype(F32)).astype(BF16)


def basis(x):
    s = x * x
    outer = s * (9 / 16) - (1 / 16)
    inner = s * (27 / 16) - (27 / 16)
    ends, mids = outer * x, inner * x
    third = inner * (1 / 3)
    return [outer - ends, mids - third, -(mids + third), outer + ends]


def pairs(tiles):
    return [cat(tiles[i:i + 2], axis=0) for i in range(0, len(tiles), 2)]


def split_tiles(tiles):
    both = [split(p) for p in pairs(tiles)]
    return cat([b[0] for b in both], axis=0), cat([b[1] for b in both], axis=0)


def ones_where(shape, same):
    r = lax.broadcasted_iota(jnp.int32, shape, 0)
    c = lax.broadcasted_iota(jnp.int32, shape, 1)
    return jnp.where(same(r, c), 1.0, 0.0)


def drag_kernel(unroll, elem, fill, fluid, mass, pos, vel, relax, coupled, pout,
                nodal, state, acc, s_basis, s_nodal, s_first):
    diag = ones_where((BINS, 128), lambda r, c: r % 8 == c % 8)
    column = jnp.broadcast_to(elem[...].astype(F32), (128, BINS)).T
    column = cat([column, column], axis=1)
    got = jnp.zeros((2 * BINS, BINS), F32)
    cells = lax.broadcasted_iota(jnp.int32, (256, BINS), 0)
    for r in range(8):
        hot = jnp.where(cells + r * 256 == elem[...], 1.0, 0.0).astype(BF16)
        got += dot(cat(split(fluid[:, r, :]), axis=0), hot)
    got = cat([got[:BINS].T, got[BINS:].T], axis=0).astype(BF16)
    mask = diag.astype(BF16)
    for cp in range(6):
        rep = ones_where((BINS, 256), lambda r, c: r == (2 * cp + c // 128) * 16 + (c % 128) // 8).astype(BF16)
        wide = dot(got, rep)
        tile = []
        for k in range(2):
            part = wide[k * BINS:(k + 1) * BINS]
            two = [(part[:, 128 * j:128 * j + 128] * diag).reshape(GROUPS, 8, 128) for j in range(2)]
            tile.append(cat(two, axis=1).astype(BF16))
        nodal[:, cp * 16:cp * 16 + 16, 0:128] = tile[0]
        nodal[:, cp * 16:cp * 16 + 16, 128:256] = tile[0]
        nodal[:, cp * 16:cp * 16 + 16, 256:384] = tile[1]
    slots = lax.broadcasted_iota(jnp.int32, (128, BINS), 0)
    occ = jnp.where(slots < fill[...], 1.0, 0.0).T
    state[0:3] = pos[...]
    state[3:6] = vel[...]
    state[6] = relax[...] * occ
    state[7] = occ
    acc[...] = jnp.zeros_like(acc)

    def first(g, slot):
        rows = pl.ds(pl.multiple_of(g * 8, 8), 8)
        l0, l1, l2 = (basis(state[i, rows, :]) for i in range(3))
        lh, ll = split_tiles([b * c for b in l1 for c in l2])
        for a in range(4):
            s_first[slot, a] = l0[a]
        s_basis[slot, 0:128] = lh
        s_basis[slot, 128:256] = ll
        s_nodal[slot] = dot(nodal[g], cat([lh, ll, lh], axis=0))

    def second(g, slot):
        rows = pl.ds(pl.multiple_of(g * 8, 8), 8)
        x = [state[i, rows, :] for i in range(3)]
        v = [state[3 + i, rows, :] for i in range(3)]
        ro, oc = state[6, rows, :], state[7, rows, :]
        l0 = [s_first[slot, a] for a in range(4)]
        stride = oc * 0.05
        forces = []
        for c in range(3):
            t = [l0[a] * s_nodal[slot, (4 * c + a) * 8:(4 * c + a) * 8 + 8] for a in range(4)]
            dv = ro * (((t[0] + t[1]) + (t[2] + t[3])) - v[c])
            nv = v[c] + dv
            state[3 + c, rows, :] = nv
            state[c, rows, :] = jnp.clip(x[c] + stride * nv, -1.0, 1.0)
            forces += [dv * l0[a] for a in range(4)]
        fh, fl = split_tiles(forces)
        wa = cat([p.astype(BF16) for p in pairs([oc * (l * l) for l in l0])], axis=0)
        lt, llt = s_basis[slot, 0:128].T, s_basis[slot, 128:256].T
        acc[g, 0:96] += dot(cat([fh, fl, fh], axis=1), cat([lt, lt, llt], axis=0))
        acc[g, 96:128] += dot(wa, lt * lt)

    blocks = GROUPS // unroll

    def run(stage, i, side):
        for j in range(unroll):
            stage(lax.rem(i, blocks) * unroll + j, side * unroll + j)

    run(first, 0, 0)

    def body(k, _):
        i = 2 * k
        run(first, i + 1, 1)
        run(second, i, 0)
        run(first, i + 2, 0)
        run(second, i + 1, 1)
        return 0

    n = SUBSTEPS * blocks
    lax.fori_loop(0, n // 2 - 1, body, 0)
    run(first, n - 1, 1)
    run(second, n - 2, 0)
    run(second, n - 1, 1)
    pout[...] = state[0:6]
    sums = jnp.zeros((2 * BINS, 256), F32)
    for cp in range(8):
        two = cat([acc[:, (2 * cp + j) * 8:(2 * cp + j) * 8 + 8, :].reshape(BINS, 128) * diag for j in range(2)], axis=1)
        rep = ones_where((256, 256), lambda r, c: c == (2 * cp + r // 128) * 16 + (r % 128) // 8).astype(BF16)
        sums += dot(cat(split(two), axis=0), rep)
    sums = cat(split((sums[:BINS] + sums[BINS:]).T), axis=1)
    lanes = lax.broadcasted_iota(jnp.int32, (BINS, 256), 1).astype(F32)
    for r in range(8):
        hot = jnp.where(column == lanes + float(r * 256), 1.0, 0.0).astype(BF16)
        dep = dot(sums, cat([hot, hot], axis=0))
        inv = 1.0 / (mass[r:r + 1, :] + dep[192:256])
        for c in range(3):
            s = slice(c * 64, c * 64 + 64)
            coupled[s, r, :] = fluid[s, r, :] - dep[s] * inv


def drag(fluid, mass, pos, vel, relax, elem, fill, unroll=4):
    vm = pl.BlockSpec(memory_space=pltpu.VMEM)
    return pl.pallas_call(
        functools.partial(drag_kernel, unroll),
        out_shape=(jax.ShapeDtypeStruct((192, 8, 256), F32), jax.ShapeDtypeStruct((6, BINS, 128), F32)),
        in_specs=[vm] * 7,
        out_specs=(vm, vm),
        scratch_shapes=[pltpu.VMEM((GROUPS, 96, 384), BF16), pltpu.VMEM((8, BINS, 128), F32),
                        pltpu.VMEM((GROUPS, 128, 128), F32), pltpu.VMEM((2 * unroll, 256, 128), BF16),
                        pltpu.VMEM((2 * unroll, 96, 128), F32), pltpu.VMEM((2 * unroll, 4, 8, 128), F32)],
        compiler_params=pltpu.CompilerParams(vmem_limit_bytes=56 * 2**20),
    )(elem.reshape(1, BINS), fill.reshape(1, BINS), fluid, mass, pos, vel, relax)


PASSES = 4
MESH = pl.DeviceIdType.MESH


def curvature(line):
    low = line[0] - 2.0 * line[1] + line[2]
    high = line[1] - 2.0 * line[2] + line[3]
    step = low - high
    return [low + step, low, high, high - step]


CURVE = ((-2, 3, -1), (-1, 1, 0), (0, -1, 1), (1, -3, 2))
SLOPE = ((11, -7, 2), (2, 5, -1), (-1, 5, 2), (2, -7, 11))


def section_phase(src, dst, visc, sub):
    up = jnp.where(sub == 7, 0.0, 0.25)
    down = jnp.where(sub == 0, 0.0, 0.25)

    def body(i, _):
        base = pl.multiple_of(i * 16, 16)
        t = [[src[base + 4 * b + c] for c in range(4)] for b in range(4)]
        across = [curvature([t[b][c] for b in range(4)]) for c in range(4)]
        for b in range(4):
            along = curvature(t[b])
            for c in range(4):
                new = t[b][c] + visc * (along[c] + across[c][b])
                if b == 3:
                    new = new - 0.25 * t[3][c] + up * pltpu.roll(t[0][c], 7, 0)
                if b == 0:
                    new = new - 0.25 * t[0][c] + down * pltpu.roll(t[3][c], 1, 0)
                dst[base + 4 * b + c] = new
        return 0

    lax.fori_loop(0, 12, body, 0)


def airway_phase(src, dst, mix, lane):
    fore = jnp.where(lane == 255, 0.0, 0.25)
    back = jnp.where(lane == 0, 0.0, 0.25)

    def body(i, _):
        base = (i // 4) * 64 + (i % 4) * 4
        for c in range(4):
            at = [base + 16 * a + c for a in range(4)]
            q = [src[n] for n in at]
            d = [q[k + 1] - q[k] for k in range(3)]
            for a in range(4):
                new = dst[at[a]] + mix[3 * a] * d[0] + mix[3 * a + 1] * d[1] + mix[3 * a + 2] * d[2]
                if a == 3:
                    new = new - 0.25 * q[3] + fore * pltpu.roll(q[0], 255, 1)
                if a == 0:
                    new = new - 0.25 * q[0] + back * pltpu.roll(q[3], 1, 1)
                dst[at[a]] = new
        return 0

    lax.fori_loop(0, 12, body, 0)


def air_nodes(a):
    return [comp * 64 + a * 16 + k for comp in range(3) for k in range(16)]


def sec_nodes(b):
    return [comp * 64 + a * 16 + b * 4 + c for comp in range(3) for a in range(4) for c in range(4)]


def fluid_kernel(field, viscosity, speed, out, ping, pong, mix, s_sec, s_air, r_sec, r_air, send_sem, recv_sem):
    me_a, me_s = lax.axis_index("airway"), lax.axis_index("section")
    n_a, n_s = lax.axis_size("airway"), lax.axis_size("section")
    peers = [(me_a, lax.rem(me_s + 1, n_s)), (me_a, lax.rem(me_s + n_s - 1, n_s)),
             (lax.rem(me_a + 1, n_a), me_s), (lax.rem(me_a + n_a - 1, n_a), me_s)]
    barrier = pltpu.get_barrier_semaphore()
    for p in peers:
        pl.semaphore_signal(barrier, inc=1, device_id=p, device_id_type=MESH)
    visc = viscosity[...] * 2.25
    quarter = speed[...] * 0.25
    for a in range(4):
        for k in range(3):
            mix[3 * a + k] = CURVE[a][k] * visc - SLOPE[a][k] * quarter
    sub = lax.broadcasted_iota(jnp.int32, (8, 256), 0)
    lane = lax.broadcasted_iota(jnp.int32, (8, 256), 1)
    lane1 = lax.broadcasted_iota(jnp.int32, (8, 128), 1)
    some = lambda cond: jnp.where(cond, 0.25, 0.0).astype(F32)
    next_s, prev_s = some(me_s < n_s - 1), some(me_s > 0)
    next_a, prev_a = some(me_a < n_a - 1), some(me_a > 0)
    pl.semaphore_wait(barrier, 4)
    bufs = [field, ping, pong, ping, out]
    for p in range(PASSES):
        src, dst = bufs[p], bufs[p + 1]
        for slot, row, b in ((0, 7, 3), (1, 0, 0)):
            for j, n in enumerate(sec_nodes(b)):
                s_sec[p, slot, j:j + 1, :] = src[n, row:row + 1, :]
        for slot, base, a in ((0, 128, 3), (1, 0, 0)):
            packed = jnp.zeros((8, 128), F32)
            col = 127 if slot == 0 else 0
            for j, n in enumerate(air_nodes(a)):
                moved = pltpu.roll(src[n, :, base:base + 128], (j - col) % 128, 1)
                packed = jnp.where(lane1 == j, moved, packed)
            s_air[p, slot] = packed
        copies = []
        for k in range(4):
            s, r = (s_sec, r_sec) if k < 2 else (s_air, r_air)
            copies.append(pltpu.make_async_remote_copy(
                src_ref=s.at[p, k % 2], dst_ref=r.at[p, k % 2], send_sem=send_sem.at[p, k], recv_sem=recv_sem.at[p, k],
                device_id=peers[k], device_id_type=MESH))
            copies[-1].start()
        section_phase(src, dst, visc, sub)
        airway_phase(src, dst, mix, lane)
        for c in copies:
            c.wait()
        for slot, row, b, scale in ((0, 0, 0, prev_s), (1, 7, 3, next_s)):
            for j, n in enumerate(sec_nodes(b)):
                dst[n, row:row + 1, :] += scale * r_sec[p, slot, j:j + 1, :]
        for slot, base, a, scale in ((0, 0, 0, prev_a), (1, 128, 3, next_a)):
            col = 0 if slot == 0 else 127
            packed = r_air[p, slot] * scale
            for j, n in enumerate(air_nodes(a)):
                moved = pltpu.roll(packed, (col - j) % 128, 1)
                dst[n, :, base:base + 128] += jnp.where(lane1 == col, moved, 0.0)


def advance(field, viscosity, speed):
    vm = pl.BlockSpec(memory_space=pltpu.VMEM)
    return pl.pallas_call(
        fluid_kernel,
        out_shape=jax.ShapeDtypeStruct((192, 8, 256), F32),
        in_specs=[vm] * 3,
        out_specs=vm,
        scratch_shapes=[pltpu.VMEM((192, 8, 256), F32), pltpu.VMEM((192, 8, 256), F32), pltpu.VMEM((12, 8, 256), F32),
                        pltpu.VMEM((PASSES, 2, 48, 256), F32), pltpu.VMEM((PASSES, 2, 8, 128), F32),
                        pltpu.VMEM((PASSES, 2, 48, 256), F32), pltpu.VMEM((PASSES, 2, 8, 128), F32),
                        pltpu.SemaphoreType.DMA((PASSES, 4)), pltpu.SemaphoreType.DMA((PASSES, 4))],
        compiler_params=pltpu.CompilerParams(collective_id=0, has_side_effects=True, vmem_limit_bytes=56 * 2**20),
    )(field, viscosity, speed)

def local(fluid_velocity, viscosity, axial_speed, fluid_mass, positions, velocities, relax_rates, bin_element, bin_fill):
    field = fluid_velocity.reshape(192, 8, 256)
    coupled, moved = drag(field, fluid_mass, positions.transpose(1, 0, 2), velocities.transpose(1, 0, 2), relax_rates,
                          bin_element, bin_fill, 12)
    return advance(coupled, viscosity, axial_speed).reshape(fluid_velocity.shape), moved.transpose(1, 0, 2)


def solution(mesh):
    bins = ("airway", "section")
    cells = P("section", "airway")
    return jax.shard_map(
        local,
        mesh=mesh,
        in_specs=(P(None, None, *cells), cells, cells, cells, P(bins, None, None), P(bins, None, None), P(bins, None),
                  P(bins), P(bins)),
        out_specs=(P(None, None, *cells), P(bins, None, None)),
        check_vma=False,
    )
```

```python
import functools
import jax, jax.numpy as jnp, numpy as np
from jax import lax
from jax.experimental import pallas as pl
from jax.experimental.pallas import tpu as pltpu
from jax.sharding import PartitionSpec as P

F32, BF16 = jnp.float32, jnp.bfloat16
BINS, GROUPS, SUBSTEPS = 192, 24, 16
cat = jnp.concatenate


def dot(a, b):
    return jnp.dot(a, b, preferred_element_type=F32)


def split(x):
    hi = x.astype(BF16)
    return hi, (x - hi.astype(F32)).astype(BF16)


def basis(x):
    s = x * x
    outer = s * (9 / 16) - (1 / 16)
    inner = s * (27 / 16) - (27 / 16)
    ends, mids = outer * x, inner * x
    third = inner * (1 / 3)
    return [outer - ends, mids - third, -(mids + third), outer + ends]


def pairs(tiles):
    return [cat(tiles[i:i + 2], axis=0) for i in range(0, len(tiles), 2)]


def split_tiles(tiles):
    both = [split(p) for p in pairs(tiles)]
    return cat([b[0] for b in both], axis=0), cat([b[1] for b in both], axis=0)


def ones_where(shape, same):
    r = lax.broadcasted_iota(jnp.int32, shape, 0)
    c = lax.broadcasted_iota(jnp.int32, shape, 1)
    return jnp.where(same(r, c), 1.0, 0.0)


def drag_kernel(unroll, elem, fill, fluid, mass, pos, vel, relax, coupled, pout,
                nodal, state, acc, s_basis, s_nodal, s_first):
    diag = ones_where((BINS, 128), lambda r, c: r % 8 == c % 8)
    column = jnp.broadcast_to(elem[...].astype(F32), (128, BINS)).T
    column = cat([column, column], axis=1)
    got = jnp.zeros((2 * BINS, BINS), F32)
    cells = lax.broadcasted_iota(jnp.int32, (256, BINS), 0)
    for r in range(8):
        hot = jnp.where(cells + r * 256 == elem[...], 1.0, 0.0).astype(BF16)
        got += dot(cat(split(cat([fluid[pl.ds(8 * h + r, BINS, stride=16), :] for h in range(2)], axis=1)), axis=0), hot)
    got = cat([got[:BINS].T, got[BINS:].T], axis=0).astype(BF16)
    mask = diag.astype(BF16)
    for cp in range(6):
        rep = ones_where((BINS, 256), lambda r, c: r == cp * 32 + (c >> 3)).astype(BF16)
        wide = dot(got, rep)
        tile = []
        for k in range(2):
            part = wide[k * BINS:(k + 1) * BINS]
            two = [(part[:, 128 * j:128 * j + 128] * diag).reshape(GROUPS, 8, 128) for j in range(2)]
            tile.append(cat(two, axis=1).astype(BF16))
        nodal[:, cp * 16:cp * 16 + 16, 0:128] = tile[0]
        nodal[:, cp * 16:cp * 16 + 16, 128:256] = tile[0]
        nodal[:, cp * 16:cp * 16 + 16, 256:384] = tile[1]
    slots = lax.broadcasted_iota(jnp.int32, (128, BINS), 0)
    occ = jnp.where(slots < fill[...], 1.0, 0.0).T
    state[0:3] = pos[...]
    state[3:6] = vel[...]
    state[6] = relax[...] * occ
    state[7] = occ
    acc[...] = jnp.zeros_like(acc)

    def first(g, slot):
        rows = pl.ds(pl.multiple_of(g * 8, 8), 8)
        l0, l1, l2 = (basis(state[i, rows, :]) for i in range(3))
        lh, ll = split_tiles([b * c for b in l1 for c in l2])
        for a in range(4):
            s_first[slot, a] = l0[a]
        s_basis[slot, 0:128] = lh
        s_basis[slot, 128:256] = ll
        s_nodal[slot] = dot(nodal[g], cat([lh, ll, lh], axis=0))

    def second(g, slot):
        rows = pl.ds(pl.multiple_of(g * 8, 8), 8)
        x = [state[i, rows, :] for i in range(3)]
        v = [state[3 + i, rows, :] for i in range(3)]
        ro, oc = state[6, rows, :], state[7, rows, :]
        l0 = [s_first[slot, a] for a in range(4)]
        stride = oc * 0.05
        forces = []
        for c in range(3):
            t = [l0[a] * s_nodal[slot, (4 * c + a) * 8:(4 * c + a) * 8 + 8] for a in range(4)]
            dv = ro * (((t[0] + t[1]) + (t[2] + t[3])) - v[c])
            nv = v[c] + dv
            state[3 + c, rows, :] = nv
            state[c, rows, :] = jnp.clip(x[c] + stride * nv, -1.0, 1.0)
            forces += [dv * l0[a] for a in range(4)]
        fh, fl = split_tiles(forces)
        wa = cat([p.astype(BF16) for p in pairs([oc * (l * l) for l in l0])], axis=0)
        lt, llt = s_basis[slot, 0:128].T, s_basis[slot, 128:256].T
        acc[g, 0:96] += dot(cat([fh, fl, fh], axis=1), cat([lt, lt, llt], axis=0))
        acc[g, 96:128] += dot(wa, lt * lt)

    blocks = GROUPS // unroll

    def run(stage, i, side):
        for j in range(unroll):
            stage(lax.rem(i, blocks) * unroll + j, side * unroll + j)

    run(first, 0, 0)

    def body(k, _):
        i = 2 * k
        run(first, i + 1, 1)
        run(second, i, 0)
        run(first, i + 2, 0)
        run(second, i + 1, 1)
        return 0

    n = SUBSTEPS * blocks
    lax.fori_loop(0, n // 2 - 1, body, 0)
    run(first, n - 1, 1)
    run(second, n - 2, 0)
    run(second, n - 1, 1)
    pout[...] = state[0:6]
    sums = jnp.zeros((2 * BINS, 256), F32)
    for cp in range(8):
        two = cat([acc[:, (2 * cp + j) * 8:(2 * cp + j) * 8 + 8, :].reshape(BINS, 128) * diag for j in range(2)], axis=1)
        rep = ones_where((256, 256), lambda r, c: c == cp * 32 + (r >> 3)).astype(BF16)
        sums += dot(cat(split(two), axis=0), rep)
    sums = cat(split((sums[:BINS] + sums[BINS:]).T), axis=1)
    lanes = lax.broadcasted_iota(jnp.int32, (BINS, 256), 1).astype(F32)
    for r in range(8):
        hot = jnp.where(column == lanes + float(r * 256), 1.0, 0.0).astype(BF16)
        dep = dot(sums, cat([hot, hot], axis=0))
        inv = 1.0 / (mass[r:r + 1, :] + dep[192:256])
        for c in range(3):
            change = dep[c * 64:c * 64 + 64] * inv
            for h in range(2):
                s = pl.ds(c * 1024 + 8 * h + r, 64, stride=16)
                coupled[s, :] = fluid[s, :] - change[:, 128 * h:128 * h + 128]


def drag(*a, **k):
    q, p = drag_(*a, **k)
    return q.reshape(192, 2, 8, 128).transpose(0, 2, 1, 3).reshape(192, 8, 256), p


def drag_(fluid, mass, pos, vel, relax, elem, fill, unroll=4):
    vm = pl.BlockSpec(memory_space=pltpu.VMEM)
    return pl.pallas_call(
        functools.partial(drag_kernel, unroll),
        out_shape=(jax.ShapeDtypeStruct((3072, 128), F32), jax.ShapeDtypeStruct((6, BINS, 128), F32)),
        in_specs=[vm] * 7,
        out_specs=(vm, vm),
        scratch_shapes=[pltpu.VMEM((GROUPS, 96, 384), BF16), pltpu.VMEM((8, BINS, 128), F32),
                        pltpu.VMEM((GROUPS, 128, 128), F32), pltpu.VMEM((2 * unroll, 256, 128), BF16),
                        pltpu.VMEM((2 * unroll, 96, 128), F32), pltpu.VMEM((2 * unroll, 4, 8, 128), F32)],
        compiler_params=pltpu.CompilerParams(vmem_limit_bytes=56 * 2**20),
    )(elem.reshape(1, BINS), fill.reshape(1, BINS), fluid.reshape(192, 8, 2, 128).transpose(0, 2, 1, 3).reshape(3072, 128), mass, pos, vel, relax)


PASSES = 4
MESH = pl.DeviceIdType.MESH


def curvature(line):
    low = line[0] - 2.0 * line[1] + line[2]
    high = line[1] - 2.0 * line[2] + line[3]
    step = low - high
    return [low + step, low, high, high - step]


CURVE = ((-2, 3, -1), (-1, 1, 0), (0, -1, 1), (1, -3, 2))
SLOPE = ((11, -7, 2), (2, 5, -1), (-1, 5, 2), (2, -7, 11))


def section_phase(src, dst, visc, sub, comp):
    up = jnp.where(sub == 7, 0.0, 0.25)
    down = jnp.where(sub == 0, 0.0, 0.25)

    def body(i, _):
        base = comp * 64 + i * 16
        t = [[src[base + 4 * b + c] for c in range(4)] for b in range(4)]
        across = [curvature([t[b][c] for b in range(4)]) for c in range(4)]
        for b in range(4):
            along = curvature(t[b])
            for c in range(4):
                new = t[b][c] + visc * (along[c] + across[c][b])
                if b == 3:
                    new = new - 0.25 * t[3][c] + up * pltpu.roll(t[0][c], 7, 0)
                if b == 0:
                    new = new - 0.25 * t[0][c] + down * pltpu.roll(t[3][c], 1, 0)
                dst[base + 4 * b + c] = new
        return 0

    lax.fori_loop(0, 4, body, 0, unroll=2)


def airway_phase(src, dst, mix, lane, comp):
    fore = jnp.where(lane == 255, 0.0, 0.25)
    back = jnp.where(lane == 0, 0.0, 0.25)

    def body(i, _):
        base = comp * 64 + i * 4
        for c in range(4):
            at = [base + 16 * a + c for a in range(4)]
            q = [src[n] for n in at]
            d = [q[k + 1] - q[k] for k in range(3)]
            for a in range(4):
                new = dst[at[a]] + mix[3 * a] * d[0] + mix[3 * a + 1] * d[1] + mix[3 * a + 2] * d[2]
                if a == 3:
                    new = new - 0.25 * q[3] + fore * pltpu.roll(q[0], 255, 1)
                if a == 0:
                    new = new - 0.25 * q[0] + back * pltpu.roll(q[3], 1, 1)
                dst[at[a]] = new
        return 0

    lax.fori_loop(0, 4, body, 0, unroll=2)


def air_nodes(a, comp):
    return [comp * 64 + a * 16 + k for k in range(16)]


def sec_nodes(b, comp):
    return [comp * 64 + a * 16 + b * 4 + c for a in range(4) for c in range(4)]


def fluid_kernel(field, viscosity, speed, out, ping, pong, mix, s_sec, s_air, r_sec, r_air, send_sem, recv_sem):
    me_a, me_s = lax.axis_index("airway"), lax.axis_index("section")
    n_a, n_s = lax.axis_size("airway"), lax.axis_size("section")
    peers = [(me_a, lax.rem(me_s + 1, n_s)), (me_a, lax.rem(me_s + n_s - 1, n_s)),
             (lax.rem(me_a + 1, n_a), me_s), (lax.rem(me_a + n_a - 1, n_a), me_s)]
    barrier = pltpu.get_barrier_semaphore()
    for p in peers:
        pl.semaphore_signal(barrier, inc=1, device_id=p, device_id_type=MESH)
    visc = viscosity[...] * 2.25
    quarter = speed[...] * 0.25
    for a in range(4):
        for k in range(3):
            mix[3 * a + k] = CURVE[a][k] * visc - SLOPE[a][k] * quarter
    sub = lax.broadcasted_iota(jnp.int32, (8, 256), 0)
    lane = lax.broadcasted_iota(jnp.int32, (8, 256), 1)
    lane1 = lax.broadcasted_iota(jnp.int32, (8, 128), 1)
    some = lambda cond: jnp.where(cond, 0.25, 0.0).astype(F32)
    next_s, prev_s = some(me_s < n_s - 1), some(me_s > 0)
    next_a, prev_a = some(me_a < n_a - 1), some(me_a > 0)
    pl.semaphore_wait(barrier, 4)
    bufs = [field, ping, pong, ping, out]
    flying = {}

    def send(p, comp):
        src = bufs[p]
        for slot, row, b in ((0, 7, 3), (1, 0, 0)):
            for j, n in enumerate(sec_nodes(b, comp)):
                s_sec[p, comp, slot, j:j + 1, :] = src[n, row:row + 1, :]
        copies = [start(p, comp, k, s_sec, r_sec) for k in (0, 1)]
        for slot, base, a in ((0, 128, 3), (1, 0, 0)):
            packed = jnp.zeros((8, 128), F32)
            col = 127 if slot == 0 else 0
            for j, n in enumerate(air_nodes(a, comp)):
                moved = pltpu.roll(src[n, :, base:base + 128], (j - col) % 128, 1)
                packed = jnp.where(lane1 == j, moved, packed)
            s_air[p, comp, slot] = packed
        flying[p, comp] = copies + [start(p, comp, k, s_air, r_air) for k in (2, 3)]

    def start(p, comp, k, s, r):
        copy = pltpu.make_async_remote_copy(
            src_ref=s.at[p, comp, k % 2], dst_ref=r.at[p, comp, k % 2], send_sem=send_sem.at[p, comp, k],
            recv_sem=recv_sem.at[p, comp, k], device_id=peers[k], device_id_type=MESH)
        copy.start()
        return copy

    def receive(p, comp):
        dst = bufs[p + 1]
        for c in flying[p, comp]:
            c.wait()
        for slot, row, b, scale in ((0, 0, 0, prev_s), (1, 7, 3, next_s)):
            for j, n in enumerate(sec_nodes(b, comp)):
                dst[n, row:row + 1, :] += scale * r_sec[p, comp, slot, j:j + 1, :]
        for slot, base, a, scale in ((0, 0, 0, prev_a), (1, 128, 3, next_a)):
            col = 0 if slot == 0 else 127
            packed = r_air[p, comp, slot] * scale
            for j, n in enumerate(air_nodes(a, comp)):
                moved = pltpu.roll(packed, (col - j) % 128, 1)
                dst[n, :, base:base + 128] += jnp.where(lane1 == col, moved, 0.0)

    for p in range(PASSES):
        for comp in range(3):
            if p:
                receive(p - 1, comp)
            send(p, comp)
            section_phase(bufs[p], bufs[p + 1], visc, sub, comp)
            airway_phase(bufs[p], bufs[p + 1], mix, lane, comp)
    for comp in range(3):
        receive(PASSES - 1, comp)


def advance(field, viscosity, speed):
    vm = pl.BlockSpec(memory_space=pltpu.VMEM)
    return pl.pallas_call(
        fluid_kernel,
        out_shape=jax.ShapeDtypeStruct((192, 8, 256), F32),
        in_specs=[vm] * 3,
        out_specs=vm,
        scratch_shapes=[pltpu.VMEM((192, 8, 256), F32), pltpu.VMEM((192, 8, 256), F32), pltpu.VMEM((12, 8, 256), F32),
                        pltpu.VMEM((PASSES, 3, 2, 16, 256), F32), pltpu.VMEM((PASSES, 3, 2, 8, 128), F32),
                        pltpu.VMEM((PASSES, 3, 2, 16, 256), F32), pltpu.VMEM((PASSES, 3, 2, 8, 128), F32),
                        pltpu.SemaphoreType.DMA((PASSES, 3, 4)), pltpu.SemaphoreType.DMA((PASSES, 3, 4))],
        compiler_params=pltpu.CompilerParams(collective_id=0, has_side_effects=True, vmem_limit_bytes=56 * 2**20),
    )(field, viscosity, speed)

def local(fluid_velocity, viscosity, axial_speed, fluid_mass, positions, velocities, relax_rates, bin_element, bin_fill):
    field = fluid_velocity.reshape(192, 8, 256)
    coupled, moved = drag(field, fluid_mass, positions.transpose(1, 0, 2), velocities.transpose(1, 0, 2), relax_rates,
                          bin_element, bin_fill, 12)
    return advance(coupled, viscosity, axial_speed).reshape(fluid_velocity.shape), moved.transpose(1, 0, 2)


def solution(mesh):
    bins = ("airway", "section")
    cells = P("section", "airway")
    return jax.shard_map(
        local,
        mesh=mesh,
        in_specs=(P(None, None, *cells), cells, cells, cells, P(bins, None, None), P(bins, None, None), P(bins, None),
                  P(bins), P(bins)),
        out_specs=(P(None, None, *cells), P(bins, None, None)),
        check_vma=False,
    )
```

```python
import functools
import jax, jax.numpy as jnp, numpy as np
from jax import lax
from jax.experimental import pallas as pl
from jax.experimental.pallas import tpu as pltpu
from jax.sharding import PartitionSpec as P

F32, BF16 = jnp.float32, jnp.bfloat16
BINS, GROUPS, SUBSTEPS = 192, 24, 16
cat = jnp.concatenate


def dot(a, b):
    return jnp.dot(a, b, preferred_element_type=F32)


def split(x):
    hi = x.astype(BF16)
    return hi, (x - hi.astype(F32)).astype(BF16)


def basis(x):
    s = x * x
    outer = s * (9 / 16) - (1 / 16)
    inner = s * (27 / 16) - (27 / 16)
    ends, mids = outer * x, inner * x
    third = inner * (1 / 3)
    return [outer - ends, mids - third, -(mids + third), outer + ends]


def pairs(tiles):
    return [cat(tiles[i:i + 2], axis=0) for i in range(0, len(tiles), 2)]


def split_tiles(tiles):
    both = [split(p) for p in pairs(tiles)]
    return cat([b[0] for b in both], axis=0), cat([b[1] for b in both], axis=0)


def ones_where(shape, same):
    r = lax.broadcasted_iota(jnp.int32, shape, 0)
    c = lax.broadcasted_iota(jnp.int32, shape, 1)
    return jnp.where(same(r, c), 1.0, 0.0)


def drag_kernel(unroll, elem, fill, fluid, mass, pos, vel, relax, coupled, pout,
                nodal, state, acc, s_basis, s_nodal, s_first):
    diag = ones_where((BINS, 128), lambda r, c: r % 8 == c % 8)
    column = jnp.broadcast_to(elem[...].astype(F32), (128, BINS)).T
    column = cat([column, column], axis=1)
    got = jnp.zeros((2 * BINS, BINS), F32)
    cells = lax.broadcasted_iota(jnp.int32, (256, BINS), 0)
    for r in range(8):
        hot = jnp.where(cells + r * 256 == elem[...], 1.0, 0.0).astype(BF16)
        got += dot(cat(split(cat([fluid[pl.ds(8 * h + r, BINS, stride=16), :] for h in range(2)], axis=1)), axis=0), hot)
    got = cat([got[:BINS].T, got[BINS:].T], axis=0).astype(BF16)
    mask = diag.astype(BF16)
    for cp in range(6):
        rep = ones_where((BINS, 256), lambda r, c: r == cp * 32 + (c >> 3)).astype(BF16)
        wide = dot(got, rep)
        tile = []
        for k in range(2):
            part = wide[k * BINS:(k + 1) * BINS]
            two = [(part[:, 128 * j:128 * j + 128] * diag).reshape(GROUPS, 8, 128) for j in range(2)]
            tile.append(cat(two, axis=1).astype(BF16))
        nodal[:, cp * 16:cp * 16 + 16, 0:128] = tile[0]
        nodal[:, cp * 16:cp * 16 + 16, 128:256] = tile[0]
        nodal[:, cp * 16:cp * 16 + 16, 256:384] = tile[1]
    slots = lax.broadcasted_iota(jnp.int32, (128, BINS), 0)
    occ = jnp.where(slots < fill[...], 1.0, 0.0).T
    state[0:3] = pos[...]
    state[3:6] = vel[...]
    state[6] = relax[...] * occ
    state[7] = occ
    acc[...] = jnp.zeros_like(acc)

    def first(g, slot):
        rows = pl.ds(pl.multiple_of(g * 8, 8), 8)
        l0, l1, l2 = (basis(state[i, rows, :]) for i in range(3))
        lh, ll = split_tiles([b * c for b in l1 for c in l2])
        for a in range(4):
            s_first[slot, a] = l0[a]
        s_basis[slot, 0:128] = lh
        s_basis[slot, 128:256] = ll
        s_nodal[slot] = dot(nodal[g], cat([lh, ll, lh], axis=0))

    def second(g, slot):
        rows = pl.ds(pl.multiple_of(g * 8, 8), 8)
        x = [state[i, rows, :] for i in range(3)]
        v = [state[3 + i, rows, :] for i in range(3)]
        ro, oc = state[6, rows, :], state[7, rows, :]
        l0 = [s_first[slot, a] for a in range(4)]
        stride = oc * 0.05
        forces = []
        for c in range(3):
            t = [l0[a] * s_nodal[slot, (4 * c + a) * 8:(4 * c + a) * 8 + 8] for a in range(4)]
            dv = ro * (((t[0] + t[1]) + (t[2] + t[3])) - v[c])
            nv = v[c] + dv
            state[3 + c, rows, :] = nv
            state[c, rows, :] = jnp.clip(x[c] + stride * nv, -1.0, 1.0)
            forces += [dv * l0[a] for a in range(4)]
        fh, fl = split_tiles(forces)
        wa = cat([p.astype(BF16) for p in pairs([oc * (l * l) for l in l0])], axis=0)
        lt, llt = s_basis[slot, 0:128].T, s_basis[slot, 128:256].T
        acc[g, 0:96] += dot(cat([fh, fl, fh], axis=1), cat([lt, lt, llt], axis=0))
        acc[g, 96:128] += dot(wa, lt * lt)

    blocks = GROUPS // unroll

    def run(stage, i, side):
        for j in range(unroll):
            stage(lax.rem(i, blocks) * unroll + j, side * unroll + j)

    run(first, 0, 0)

    def body(k, _):
        i = 2 * k
        run(first, i + 1, 1)
        run(second, i, 0)
        run(first, i + 2, 0)
        run(second, i + 1, 1)
        return 0

    n = SUBSTEPS * blocks
    lax.fori_loop(0, n // 2 - 1, body, 0)
    run(first, n - 1, 1)
    run(second, n - 2, 0)
    run(second, n - 1, 1)
    pout[...] = state[0:6]
    sums = jnp.zeros((2 * BINS, 256), F32)
    for cp in range(8):
        two = cat([acc[:, (2 * cp + j) * 8:(2 * cp + j) * 8 + 8, :].reshape(BINS, 128) * diag for j in range(2)], axis=1)
        rep = ones_where((256, 256), lambda r, c: c == cp * 32 + (r >> 3)).astype(BF16)
        sums += dot(cat(split(two), axis=0), rep)
    sums = cat(split((sums[:BINS] + sums[BINS:]).T), axis=1)
    lanes = lax.broadcasted_iota(jnp.int32, (BINS, 256), 1).astype(F32)
    for r in range(8):
        hot = jnp.where(column == lanes + float(r * 256), 1.0, 0.0).astype(BF16)
        dep = dot(sums, cat([hot, hot], axis=0))
        inv = 1.0 / (mass[r:r + 1, :] + dep[192:256])
        for c in range(3):
            change = dep[c * 64:c * 64 + 64] * inv
            for h in range(2):
                s = pl.ds(c * 1024 + 8 * h + r, 64, stride=16)
                coupled[s, :] = fluid[s, :] - change[:, 128 * h:128 * h + 128]


def drag(*a, **k):
    q, p = drag_(*a, **k)
    return q.reshape(192, 2, 8, 128).transpose(0, 2, 1, 3).reshape(192, 8, 256), p


def drag_(fluid, mass, pos, vel, relax, elem, fill, unroll=4):
    vm = pl.BlockSpec(memory_space=pltpu.VMEM)
    return pl.pallas_call(
        functools.partial(drag_kernel, unroll),
        out_shape=(pltpu.VMEM((3072, 128), F32), jax.ShapeDtypeStruct((6, BINS, 128), F32)),
        in_specs=[vm] * 7,
        out_specs=(vm, vm),
        scratch_shapes=[pltpu.VMEM((GROUPS, 96, 384), BF16), pltpu.VMEM((8, BINS, 128), F32),
                        pltpu.VMEM((GROUPS, 128, 128), F32), pltpu.VMEM((2 * unroll, 256, 128), BF16),
                        pltpu.VMEM((2 * unroll, 96, 128), F32), pltpu.VMEM((2 * unroll, 4, 8, 128), F32)],
        compiler_params=pltpu.CompilerParams(vmem_limit_bytes=56 * 2**20),
    )(elem.reshape(1, BINS), fill.reshape(1, BINS), fluid.reshape(192, 8, 2, 128).transpose(0, 2, 1, 3).reshape(3072, 128), mass, pos, vel, relax)


PASSES = 4
MESH = pl.DeviceIdType.MESH


def curvature(line):
    low = line[0] - 2.0 * line[1] + line[2]
    high = line[1] - 2.0 * line[2] + line[3]
    step = low - high
    return [low + step, low, high, high - step]


CURVE = ((-2, 3, -1), (-1, 1, 0), (0, -1, 1), (1, -3, 2))
SLOPE = ((11, -7, 2), (2, 5, -1), (-1, 5, 2), (2, -7, 11))


def section_phase(src, dst, visc, sub, comp):
    up = jnp.where(sub == 7, 0.0, 0.25)
    down = jnp.where(sub == 0, 0.0, 0.25)

    def body(i, _):
        base = comp * 64 + i * 16
        t = [[src[base + 4 * b + c] for c in range(4)] for b in range(4)]
        across = [curvature([t[b][c] for b in range(4)]) for c in range(4)]
        for b in range(4):
            along = curvature(t[b])
            for c in range(4):
                new = t[b][c] + visc * (along[c] + across[c][b])
                if b == 3:
                    new = new - 0.25 * t[3][c] + up * pltpu.roll(t[0][c], 7, 0)
                if b == 0:
                    new = new - 0.25 * t[0][c] + down * pltpu.roll(t[3][c], 1, 0)
                dst[base + 4 * b + c] = new
        return 0

    lax.fori_loop(0, 4, body, 0, unroll=2)


def airway_phase(src, dst, mix, lane, comp):
    fore = jnp.where(lane == 255, 0.0, 0.25)
    back = jnp.where(lane == 0, 0.0, 0.25)

    def body(i, _):
        base = comp * 64 + i * 4
        for c in range(4):
            at = [base + 16 * a + c for a in range(4)]
            q = [src[n] for n in at]
            d = [q[k + 1] - q[k] for k in range(3)]
            for a in range(4):
                new = dst[at[a]] + mix[3 * a] * d[0] + mix[3 * a + 1] * d[1] + mix[3 * a + 2] * d[2]
                if a == 3:
                    new = new - 0.25 * q[3] + fore * pltpu.roll(q[0], 255, 1)
                if a == 0:
                    new = new - 0.25 * q[0] + back * pltpu.roll(q[3], 1, 1)
                dst[at[a]] = new
        return 0

    lax.fori_loop(0, 4, body, 0, unroll=2)


def air_nodes(a, comp):
    return [comp * 64 + a * 16 + k for k in range(16)]


def sec_nodes(b, comp):
    return [comp * 64 + a * 16 + b * 4 + c for a in range(4) for c in range(4)]


def fluid_kernel(field, viscosity, speed, out, ping, pong, mix, s_sec, s_air, r_sec, r_air, s_cor, r_cor, send_sem,
                 recv_sem):
    me_a, me_s = lax.axis_index("airway"), lax.axis_index("section")
    n_a, n_s = lax.axis_size("airway"), lax.axis_size("section")
    peers = [(me_a, lax.rem(me_s + 1, n_s)), (me_a, lax.rem(me_s + n_s - 1, n_s)),
             (lax.rem(me_a + 1, n_a), me_s), (lax.rem(me_a + n_a - 1, n_a), me_s)]
    peers += [(peers[2 + a][0], peers[b][1]) for b in range(2) for a in range(2)]
    barrier = pltpu.get_barrier_semaphore()
    for p in peers:
        pl.semaphore_signal(barrier, inc=1, device_id=p, device_id_type=MESH)
    visc = viscosity[...] * 2.25
    quarter = speed[...] * 0.25
    for a in range(4):
        for k in range(3):
            mix[3 * a + k] = CURVE[a][k] * visc - SLOPE[a][k] * quarter
    sub = lax.broadcasted_iota(jnp.int32, (8, 256), 0)
    lane = lax.broadcasted_iota(jnp.int32, (8, 256), 1)
    lane1 = lax.broadcasted_iota(jnp.int32, (8, 128), 1)
    sub1 = lax.broadcasted_iota(jnp.int32, (8, 128), 0)
    some = lambda cond: jnp.where(cond, 0.25, 0.0).astype(F32)
    next_s, prev_s = some(me_s < n_s - 1), some(me_s > 0)
    next_a, prev_a = some(me_a < n_a - 1), some(me_a > 0)
    pl.semaphore_wait(barrier, 8)
    bufs = [field, ping, pong, ping, out]
    flying = {}

    def send(p, comp):
        src = bufs[p]
        for slot, row, b in ((0, 7, 3), (1, 0, 0)):
            for j, n in enumerate(sec_nodes(b, comp)):
                s_sec[p, comp, slot, j:j + 1, :] = src[n, row:row + 1, :]
        copies = [start(p, comp, k, s_sec.at[p, comp, k], r_sec.at[p, comp, k]) for k in range(2)]
        for slot, base, a in ((0, 128, 3), (1, 0, 0)):
            packed = jnp.zeros((8, 128), F32)
            col = 127 if slot == 0 else 0
            for j, n in enumerate(air_nodes(a, comp)):
                moved = pltpu.roll(src[n, :, base:base + 128], (j - col) % 128, 1)
                packed = jnp.where(lane1 == j, moved, packed)
            s_air[p, comp, slot] = packed
        copies += [start(p, comp, 2 + k, s_air.at[p, comp, k], r_air.at[p, comp, k]) for k in range(2)]
        if p % 2 == 0:
            for b in range(2):
                for a in range(2):
                    rows = s_sec[p, comp, b, 12 - 12 * a:16 - 12 * a, (1 - a) * 128:(2 - a) * 128]
                    rows = pltpu.roll(cat([rows, rows], axis=0), 1 if a == 0 else 127, 1)
                    s_cor[p // 2, comp, 2 * b + a, 0] = jnp.where(lane1 == 127 * a, rows, 0.0)
                    tile = pltpu.roll(s_air[p, comp, a], 1 if b == 0 else 7, 0)
                    tile = pltpu.roll(tile, 116 if b == 0 else 12, 1)
                    hit = (sub1 == 7 * b) & (lane1 // 4 == 3 * b)
                    s_cor[p // 2, comp, 2 * b + a, 1] = jnp.where(hit, tile, 0.0)
                    k = 2 * b + a
                    copies.append(start(p, comp, 4 + k, s_cor.at[p // 2, comp, k], r_cor.at[p // 2, comp, k]))
        flying[p, comp] = copies

    def start(p, comp, k, s, r):
        copy = pltpu.make_async_remote_copy(
            src_ref=s, dst_ref=r, send_sem=send_sem.at[p, comp, k], recv_sem=recv_sem.at[p, comp, k],
            device_id=peers[k], device_id_type=MESH)
        copy.start()
        return copy

    def complete(p, comp):
        for c in flying[p + 1, comp]:
            c.wait()
        for c in flying[p, comp][4:]:
            c.wait()
        near = [[r_cor[p // 2, comp, 2 * b + a] for a in range(2)] for b in range(2)]
        for slot in range(2):
            r_sec[p + 1, comp, slot] += 0.25 * s_sec[p, comp, 1 - slot]
            r_air[p + 1, comp, slot] += 0.25 * s_air[p, comp, 1 - slot]
            for other in range(2):
                scale = (prev_a, next_a)[other]
                low = 12 * other
                r_sec[p + 1, comp, slot, low:low + 4, other * 128:other * 128 + 128] += scale * near[slot][other][0, 0:4]
                scale = (prev_s, next_s)[other]
                r_air[p + 1, comp, slot] += scale * near[other][slot][1]

    def receive(p, comp):
        dst = bufs[p + 1]
        if p % 2 == 0:
            for c in flying[p, comp][:4]:
                c.wait()
        else:
            complete(p - 1, comp)
        for slot, row, b, scale in ((0, 0, 0, prev_s), (1, 7, 3, next_s)):
            for j, n in enumerate(sec_nodes(b, comp)):
                dst[n, row:row + 1, :] += scale * r_sec[p, comp, slot, j:j + 1, :]
        for slot, base, a, scale in ((0, 0, 0, prev_a), (1, 128, 3, next_a)):
            col = 0 if slot == 0 else 127
            packed = r_air[p, comp, slot] * scale
            for j, n in enumerate(air_nodes(a, comp)):
                moved = pltpu.roll(packed, (col - j) % 128, 1)
                dst[n, :, base:base + 128] += jnp.where(lane1 == col, moved, 0.0)

    def advance_one(p, comp):
        section_phase(bufs[p], bufs[p + 1], visc, sub, comp)
        airway_phase(bufs[p], bufs[p + 1], mix, lane, comp)

    for p in range(0, PASSES, 2):
        for comp in range(3):
            if p:
                receive(p - 1, comp)
            send(p, comp)
            advance_one(p, comp)
            send(p + 1, comp)
        for comp in range(3):
            receive(p, comp)
            advance_one(p + 1, comp)
    for comp in range(3):
        receive(PASSES - 1, comp)


def advance(field, viscosity, speed):
    vm = pl.BlockSpec(memory_space=pltpu.VMEM)
    return pl.pallas_call(
        fluid_kernel,
        out_shape=pltpu.VMEM((192, 8, 256), F32),
        in_specs=[vm] * 3,
        out_specs=vm,
        scratch_shapes=[pltpu.VMEM((192, 8, 256), F32), pltpu.VMEM((192, 8, 256), F32), pltpu.VMEM((12, 8, 256), F32),
                        pltpu.VMEM((PASSES, 3, 2, 16, 256), F32), pltpu.VMEM((PASSES, 3, 2, 8, 128), F32),
                        pltpu.VMEM((PASSES, 3, 2, 16, 256), F32), pltpu.VMEM((PASSES, 3, 2, 8, 128), F32),
                        pltpu.VMEM((PASSES // 2, 3, 4, 2, 8, 128), F32), pltpu.VMEM((PASSES // 2, 3, 4, 2, 8, 128), F32),
                        pltpu.SemaphoreType.DMA((PASSES, 3, 8)), pltpu.SemaphoreType.DMA((PASSES, 3, 8))],
        compiler_params=pltpu.CompilerParams(collective_id=0, has_side_effects=True, vmem_limit_bytes=56 * 2**20),
    )(pltpu.with_memory_space_constraint(field, pltpu.VMEM), viscosity, speed)

def local(fluid_velocity, viscosity, axial_speed, fluid_mass, positions, velocities, relax_rates, bin_element, bin_fill):
    field = fluid_velocity.reshape(192, 8, 256)
    coupled, moved = drag(field, fluid_mass, positions.transpose(1, 0, 2), velocities.transpose(1, 0, 2), relax_rates,
                          bin_element, bin_fill, 12)
    return advance(coupled, viscosity, axial_speed).reshape(fluid_velocity.shape), moved.transpose(1, 0, 2)


def solution(mesh):
    bins = ("airway", "section")
    cells = P("section", "airway")
    return jax.shard_map(
        local,
        mesh=mesh,
        in_specs=(P(None, None, *cells), cells, cells, cells, P(bins, None, None), P(bins, None, None), P(bins, None),
                  P(bins), P(bins)),
        out_specs=(P(None, None, *cells), P(bins, None, None)),
        check_vma=False,
    )
```

```python
import functools
import jax, jax.numpy as jnp, numpy as np
from jax import lax
from jax.experimental import pallas as pl
from jax.experimental.pallas import tpu as pltpu
from jax.sharding import PartitionSpec as P

F32, BF16 = jnp.float32, jnp.bfloat16
BINS, GROUPS, SUBSTEPS = 192, 24, 16
PASSES = 4
MESH = pl.DeviceIdType.MESH
cat = jnp.concatenate


def dot(a, b):
    return jnp.dot(a, b, preferred_element_type=F32)


def split(x):
    hi = x.astype(BF16)
    return hi, (x - hi.astype(F32)).astype(BF16)


def basis(x):
    s = x * x
    outer = s * (9 / 16) - (1 / 16)
    inner = s * (27 / 16) - (27 / 16)
    ends, mids = outer * x, inner * x
    third = inner * (1 / 3)
    return [outer - ends, mids - third, -(mids + third), outer + ends]


def pairs(tiles):
    return [cat(tiles[i:i + 2], axis=0) for i in range(0, len(tiles), 2)]


def split_tiles(tiles):
    both = [split(p) for p in pairs(tiles)]
    return cat([b[0] for b in both], axis=0), cat([b[1] for b in both], axis=0)


def ones_where(shape, same):
    r = lax.broadcasted_iota(jnp.int32, shape, 0)
    c = lax.broadcasted_iota(jnp.int32, shape, 1)
    return jnp.where(same(r, c), 1.0, 0.0)


def drag_part(unroll, elem, fill, fluid, mass, pos, vel, relax, coupled, pout, nodal, state, acc, s_basis, s_nodal,
              s_first):
    diag = ones_where((BINS, 128), lambda r, c: r % 8 == c % 8)
    column = jnp.broadcast_to(elem[...].astype(F32), (128, BINS)).T
    column = cat([column, column], axis=1)
    got = jnp.zeros((2 * BINS, BINS), F32)
    cells = lax.broadcasted_iota(jnp.int32, (256, BINS), 0)
    for r in range(8):
        hot = jnp.where(cells + r * 256 == elem[...], 1.0, 0.0).astype(BF16)
        got += dot(cat(split(cat([fluid[pl.ds(8 * h + r, BINS, stride=16), :] for h in range(2)], axis=1)), axis=0), hot)
    got = cat([got[:BINS].T, got[BINS:].T], axis=0).astype(BF16)
    mask = diag.astype(BF16)
    for cp in range(6):
        rep = ones_where((BINS, 256), lambda r, c: r == cp * 32 + (c >> 3)).astype(BF16)
        wide = dot(got, rep)
        tile = []
        for k in range(2):
            part = wide[k * BINS:(k + 1) * BINS]
            two = [(part[:, 128 * j:128 * j + 128] * diag).reshape(GROUPS, 8, 128) for j in range(2)]
            tile.append(cat(two, axis=1).astype(BF16))
        nodal[:, cp * 16:cp * 16 + 16, 0:128] = tile[0]
        nodal[:, cp * 16:cp * 16 + 16, 128:256] = tile[0]
        nodal[:, cp * 16:cp * 16 + 16, 256:384] = tile[1]
    slots = lax.broadcasted_iota(jnp.int32, (128, BINS), 0)
    occ = jnp.where(slots < fill[...], 1.0, 0.0).T
    state[0:3] = pos[...]
    state[3:6] = vel[...]
    state[6] = relax[...] * occ
    state[7] = occ
    acc[...] = jnp.zeros_like(acc)

    def first(g, slot):
        rows = pl.ds(pl.multiple_of(g * 8, 8), 8)
        l0, l1, l2 = (basis(state[i, rows, :]) for i in range(3))
        lh, ll = split_tiles([b * c for b in l1 for c in l2])
        for a in range(4):
            s_first[slot, a] = l0[a]
        s_basis[slot, 0:128] = lh
        s_basis[slot, 128:256] = ll
        s_nodal[slot] = dot(nodal[g], cat([lh, ll, lh], axis=0))

    def second(g, slot):
        rows = pl.ds(pl.multiple_of(g * 8, 8), 8)
        x = [state[i, rows, :] for i in range(3)]
        v = [state[3 + i, rows, :] for i in range(3)]
        ro, oc = state[6, rows, :], state[7, rows, :]
        l0 = [s_first[slot, a] for a in range(4)]
        stride = oc * 0.05
        forces = []
        for c in range(3):
            t = [l0[a] * s_nodal[slot, (4 * c + a) * 8:(4 * c + a) * 8 + 8] for a in range(4)]
            dv = ro * (((t[0] + t[1]) + (t[2] + t[3])) - v[c])
            nv = v[c] + dv
            state[3 + c, rows, :] = nv
            state[c, rows, :] = jnp.clip(x[c] + stride * nv, -1.0, 1.0)
            forces += [dv * l0[a] for a in range(4)]
        fh, fl = split_tiles(forces)
        wa = cat([p.astype(BF16) for p in pairs([oc * (l * l) for l in l0])], axis=0)
        lt, llt = s_basis[slot, 0:128].T, s_basis[slot, 128:256].T
        acc[g, 0:96] += dot(cat([fh, fl, fh], axis=1), cat([lt, lt, llt], axis=0))
        acc[g, 96:128] += dot(wa, lt * lt)

    blocks = GROUPS // unroll

    def run(stage, i, side):
        for j in range(unroll):
            stage(lax.rem(i, blocks) * unroll + j, side * unroll + j)

    run(first, 0, 0)

    def body(k, _):
        i = 2 * k
        run(first, i + 1, 1)
        run(second, i, 0)
        run(first, i + 2, 0)
        run(second, i + 1, 1)
        return 0

    n = SUBSTEPS * blocks
    lax.fori_loop(0, n // 2 - 1, body, 0)
    run(first, n - 1, 1)
    run(second, n - 2, 0)
    run(second, n - 1, 1)
    pout[...] = state[0:6]
    sums = jnp.zeros((2 * BINS, 256), F32)
    for cp in range(8):
        two = cat([acc[:, (2 * cp + j) * 8:(2 * cp + j) * 8 + 8, :].reshape(BINS, 128) * diag for j in range(2)], axis=1)
        rep = ones_where((256, 256), lambda r, c: c == cp * 32 + (r >> 3)).astype(BF16)
        sums += dot(cat(split(two), axis=0), rep)
    sums = cat(split((sums[:BINS] + sums[BINS:]).T), axis=1)
    lanes = lax.broadcasted_iota(jnp.int32, (BINS, 256), 1).astype(F32)
    for r in range(8):
        hot = jnp.where(column == lanes + float(r * 256), 1.0, 0.0).astype(BF16)
        dep = dot(sums, cat([hot, hot], axis=0))
        inv = 1.0 / (mass[r:r + 1, :] + dep[192:256])
        for c in range(3):
            change = dep[c * 64:c * 64 + 64] * inv
            for h in range(2):
                s = pl.ds(c * 1024 + 8 * h + r, 64, stride=16)
                coupled[s, :] = fluid[s, :] - change[:, 128 * h:128 * h + 128]


def cell(src, n, rows=slice(None)):
    if src.shape[0] == BINS:
        return src[n, rows]
    return cat([src[2 * n, rows], src[2 * n + 1, rows]], axis=1)


def half(src, n, base):
    return src[n, :, base:base + 128] if src.shape[0] == BINS else src[2 * n + base // 128]


def curvature(line):
    low = line[0] - 2.0 * line[1] + line[2]
    high = line[1] - 2.0 * line[2] + line[3]
    step = low - high
    return [low + step, low, high, high - step]


CURVE = ((-2, 3, -1), (-1, 1, 0), (0, -1, 1), (1, -3, 2))
SLOPE = ((11, -7, 2), (2, 5, -1), (-1, 5, 2), (2, -7, 11))


def section_phase(src, dst, visc, sub, comp):
    up = jnp.where(sub == 7, 0.0, 0.25)
    down = jnp.where(sub == 0, 0.0, 0.25)

    def body(i, _):
        base = comp * 64 + i * 16
        t = [[cell(src, base + 4 * b + c) for c in range(4)] for b in range(4)]
        across = [curvature([t[b][c] for b in range(4)]) for c in range(4)]
        for b in range(4):
            along = curvature(t[b])
            for c in range(4):
                new = t[b][c] + visc * (along[c] + across[c][b])
                if b == 3:
                    new = new - 0.25 * t[3][c] + up * pltpu.roll(t[0][c], 7, 0)
                if b == 0:
                    new = new - 0.25 * t[0][c] + down * pltpu.roll(t[3][c], 1, 0)
                dst[base + 4 * b + c] = new
        return 0

    lax.fori_loop(0, 4, body, 0, unroll=2)


def airway_phase(src, dst, mix, lane, comp):
    fore = jnp.where(lane == 255, 0.0, 0.25)
    back = jnp.where(lane == 0, 0.0, 0.25)

    def body(i, _):
        base = comp * 64 + i * 4
        for c in range(4):
            at = [base + 16 * a + c for a in range(4)]
            q = [cell(src, n) for n in at]
            d = [q[k + 1] - q[k] for k in range(3)]
            for a in range(4):
                new = dst[at[a]] + mix[3 * a] * d[0] + mix[3 * a + 1] * d[1] + mix[3 * a + 2] * d[2]
                if a == 3:
                    new = new - 0.25 * q[3] + fore * pltpu.roll(q[0], 255, 1)
                if a == 0:
                    new = new - 0.25 * q[0] + back * pltpu.roll(q[3], 1, 1)
                dst[at[a]] = new
        return 0

    lax.fori_loop(0, 4, body, 0, unroll=2)


def air_nodes(a, comp):
    return [comp * 64 + a * 16 + k for k in range(16)]


def sec_nodes(b, comp):
    return [comp * 64 + a * 16 + b * 4 + c for a in range(4) for c in range(4)]


def kernel(unroll, elem, fill, fluid, mass, pos, vel, relax, viscosity, speed, out, pout, nodal, state, acc, s_basis,
           s_nodal, s_first, field, ping, pong, mix, s_sec, s_air, r_sec, r_air, s_cor, r_cor, send_sem, recv_sem):
    me_a, me_s = lax.axis_index("airway"), lax.axis_index("section")
    n_a, n_s = lax.axis_size("airway"), lax.axis_size("section")
    peers = [(me_a, lax.rem(me_s + 1, n_s)), (me_a, lax.rem(me_s + n_s - 1, n_s)),
             (lax.rem(me_a + 1, n_a), me_s), (lax.rem(me_a + n_a - 1, n_a), me_s)]
    peers += [(peers[2 + a][0], peers[b][1]) for b in range(2) for a in range(2)]
    barrier = pltpu.get_barrier_semaphore()
    for p in peers:
        pl.semaphore_signal(barrier, inc=1, device_id=p, device_id_type=MESH)
    drag_part(unroll, elem, fill, fluid, mass, pos, vel, relax, field.reshape(3072, 128), pout, nodal, state, acc, s_basis,
              s_nodal, s_first)
    visc = viscosity[...] * 2.25
    quarter = speed[...] * 0.25
    for a in range(4):
        for k in range(3):
            mix[3 * a + k] = CURVE[a][k] * visc - SLOPE[a][k] * quarter
    sub = lax.broadcasted_iota(jnp.int32, (8, 256), 0)
    lane = lax.broadcasted_iota(jnp.int32, (8, 256), 1)
    lane1 = lax.broadcasted_iota(jnp.int32, (8, 128), 1)
    sub1 = lax.broadcasted_iota(jnp.int32, (8, 128), 0)
    some = lambda cond: jnp.where(cond, 0.25, 0.0).astype(F32)
    next_s, prev_s = some(me_s < n_s - 1), some(me_s > 0)
    next_a, prev_a = some(me_a < n_a - 1), some(me_a > 0)
    pl.semaphore_wait(barrier, 8)
    bufs = [field, ping, pong, ping, out]
    flying = {}

    def send(p, comp):
        src = bufs[p]
        for slot, row, b in ((0, 7, 3), (1, 0, 0)):
            for j, n in enumerate(sec_nodes(b, comp)):
                s_sec[p, comp, slot, j:j + 1, :] = cell(src, n, slice(row, row + 1))
        copies = [start(p, comp, k, s_sec.at[p, comp, k], r_sec.at[p, comp, k]) for k in range(2)]
        for slot, base, a in ((0, 128, 3), (1, 0, 0)):
            packed = jnp.zeros((8, 128), F32)
            col = 127 if slot == 0 else 0
            for j, n in enumerate(air_nodes(a, comp)):
                moved = pltpu.roll(half(src, n, base), (j - col) % 128, 1)
                packed = jnp.where(lane1 == j, moved, packed)
            s_air[p, comp, slot] = packed
        copies += [start(p, comp, 2 + k, s_air.at[p, comp, k], r_air.at[p, comp, k]) for k in range(2)]
        if p % 2 == 0:
            for b in range(2):
                for a in range(2):
                    rows = s_sec[p, comp, b, 12 - 12 * a:16 - 12 * a, (1 - a) * 128:(2 - a) * 128]
                    rows = pltpu.roll(cat([rows, rows], axis=0), 1 if a == 0 else 127, 1)
                    s_cor[p // 2, comp, 2 * b + a, 0] = jnp.where(lane1 == 127 * a, rows, 0.0)
                    tile = pltpu.roll(s_air[p, comp, a], 1 if b == 0 else 7, 0)
                    tile = pltpu.roll(tile, 116 if b == 0 else 12, 1)
                    hit = (sub1 == 7 * b) & (lane1 // 4 == 3 * b)
                    s_cor[p // 2, comp, 2 * b + a, 1] = jnp.where(hit, tile, 0.0)
                    k = 2 * b + a
                    copies.append(start(p, comp, 4 + k, s_cor.at[p // 2, comp, k], r_cor.at[p // 2, comp, k]))
        flying[p, comp] = copies

    def start(p, comp, k, s, r):
        copy = pltpu.make_async_remote_copy(
            src_ref=s, dst_ref=r, send_sem=send_sem.at[p, comp, k], recv_sem=recv_sem.at[p, comp, k],
            device_id=peers[k], device_id_type=MESH)
        copy.start()
        return copy

    def complete(p, comp):
        for c in flying[p + 1, comp]:
            c.wait()
        for c in flying[p, comp][4:]:
            c.wait()
        near = [[r_cor[p // 2, comp, 2 * b + a] for a in range(2)] for b in range(2)]
        for slot in range(2):
            r_sec[p + 1, comp, slot] += 0.25 * s_sec[p, comp, 1 - slot]
            r_air[p + 1, comp, slot] += 0.25 * s_air[p, comp, 1 - slot]
            for other in range(2):
                scale = (prev_a, next_a)[other]
                low = 12 * other
                r_sec[p + 1, comp, slot, low:low + 4, other * 128:other * 128 + 128] += scale * near[slot][other][0, 0:4]
                scale = (prev_s, next_s)[other]
                r_air[p + 1, comp, slot] += scale * near[other][slot][1]

    def receive(p, comp):
        dst = bufs[p + 1]
        if p % 2 == 0:
            for c in flying[p, comp][:4]:
                c.wait()
        else:
            complete(p - 1, comp)
        for slot, row, b, scale in ((0, 0, 0, prev_s), (1, 7, 3, next_s)):
            for j, n in enumerate(sec_nodes(b, comp)):
                dst[n, row:row + 1, :] += scale * r_sec[p, comp, slot, j:j + 1, :]
        for slot, base, a, scale in ((0, 0, 0, prev_a), (1, 128, 3, next_a)):
            col = 0 if slot == 0 else 127
            packed = r_air[p, comp, slot] * scale
            for j, n in enumerate(air_nodes(a, comp)):
                moved = pltpu.roll(packed, (col - j) % 128, 1)
                dst[n, :, base:base + 128] += jnp.where(lane1 == col, moved, 0.0)

    def advance_one(p, comp):
        section_phase(bufs[p], bufs[p + 1], visc, sub, comp)
        airway_phase(bufs[p], bufs[p + 1], mix, lane, comp)

    for p in range(0, PASSES, 2):
        for comp in range(3):
            if p:
                receive(p - 1, comp)
            send(p, comp)
            advance_one(p, comp)
            send(p + 1, comp)
        for comp in range(3):
            receive(p, comp)
            advance_one(p + 1, comp)
    for comp in range(3):
        receive(PASSES - 1, comp)


def local(fluid_velocity, viscosity, axial_speed, fluid_mass, positions, velocities, relax_rates, bin_element, bin_fill):
    unroll = 12
    fluid = fluid_velocity.reshape(192, 8, 2, 128).transpose(0, 2, 1, 3).reshape(3072, 128)
    vm = pl.BlockSpec(memory_space=pltpu.VMEM)
    faces = pltpu.VMEM((PASSES, 3, 2, 16, 256), F32)
    edges = pltpu.VMEM((PASSES, 3, 2, 8, 128), F32)
    corners = pltpu.VMEM((PASSES // 2, 3, 4, 2, 8, 128), F32)
    field = pltpu.VMEM((192, 8, 256), F32)
    done, moved = pl.pallas_call(
        functools.partial(kernel, unroll),
        out_shape=(pltpu.VMEM((192, 8, 256), F32), pltpu.VMEM((6, BINS, 128), F32)),
        in_specs=[vm] * 9,
        out_specs=(vm, vm),
        scratch_shapes=[pltpu.VMEM((GROUPS, 96, 384), BF16), pltpu.VMEM((8, BINS, 128), F32),
                        pltpu.VMEM((GROUPS, 128, 128), F32), pltpu.VMEM((2 * unroll, 256, 128), BF16),
                        pltpu.VMEM((2 * unroll, 96, 128), F32), pltpu.VMEM((2 * unroll, 4, 8, 128), F32),
                        pltpu.VMEM((384, 8, 128), F32), field, field, pltpu.VMEM((12, 8, 256), F32),
                        faces, edges, faces, edges, corners, corners,
                        pltpu.SemaphoreType.DMA((PASSES, 3, 8)), pltpu.SemaphoreType.DMA((PASSES, 3, 8))],
        compiler_params=pltpu.CompilerParams(collective_id=0, has_side_effects=True, vmem_limit_bytes=52 * 2**20),
    )(bin_element.reshape(1, BINS), bin_fill.reshape(1, BINS), fluid, fluid_mass, positions.transpose(1, 0, 2),
      velocities.transpose(1, 0, 2), relax_rates, viscosity, axial_speed)
    return done.reshape(fluid_velocity.shape), moved.transpose(1, 0, 2)


def solution(mesh):
    bins = ("airway", "section")
    cells = P("section", "airway")
    return jax.shard_map(
        local,
        mesh=mesh,
        in_specs=(P(None, None, *cells), cells, cells, cells, P(bins, None, None), P(bins, None, None), P(bins, None),
                  P(bins), P(bins)),
        out_specs=(P(None, None, *cells), P(bins, None, None)),
        check_vma=False,
    )
```

```python
import functools
import jax, jax.numpy as jnp, numpy as np
from jax import lax
from jax.experimental import pallas as pl
from jax.experimental.pallas import tpu as pltpu
from jax.sharding import PartitionSpec as P

F32, BF16 = jnp.float32, jnp.bfloat16
BINS, GROUPS, SUBSTEPS = 192, 24, 16
PASSES = 4
MESH = pl.DeviceIdType.MESH
cat = jnp.concatenate


def dot(a, b):
    return jnp.dot(a, b, preferred_element_type=F32)


def split(x):
    hi = x.astype(BF16)
    return hi, (x - hi.astype(F32)).astype(BF16)


def basis(x):
    s = x * x
    outer = s * (9 / 16) - (1 / 16)
    inner = s * (27 / 16) - (27 / 16)
    ends, mids = outer * x, inner * x
    third = inner * (1 / 3)
    return [outer - ends, mids - third, -(mids + third), outer + ends]


def pairs(tiles):
    return [cat(tiles[i:i + 2], axis=0) for i in range(0, len(tiles), 2)]


def split_tiles(tiles):
    both = [split(p) for p in pairs(tiles)]
    return cat([b[0] for b in both], axis=0), cat([b[1] for b in both], axis=0)


def ones_where(shape, same):
    r = lax.broadcasted_iota(jnp.int32, shape, 0)
    c = lax.broadcasted_iota(jnp.int32, shape, 1)
    return jnp.where(same(r, c), 1.0, 0.0)


def drag_part(unroll, elem, fill, fluid, mass, pos, vel, relax, coupled, pout, nodal, state, acc, s_basis, s_nodal,
              s_first):
    diag = ones_where((BINS, 128), lambda r, c: r % 8 == c % 8)
    column = jnp.broadcast_to(elem[...].astype(F32), (128, BINS)).T
    column = cat([column, column], axis=1)
    got = jnp.zeros((2 * BINS, BINS), F32)
    cells = lax.broadcasted_iota(jnp.int32, (256, BINS), 0)
    for r in range(8):
        hot = jnp.where(cells + r * 256 == elem[...], 1.0, 0.0).astype(BF16)
        got += dot(cat(split(cat([fluid[pl.ds(8 * h + r, BINS, stride=16), :] for h in range(2)], axis=1)), axis=0), hot)
    got = cat([got[:BINS].T, got[BINS:].T], axis=0).astype(BF16)
    mask = diag.astype(BF16)
    for cp in range(6):
        rep = ones_where((BINS, 256), lambda r, c: r == cp * 32 + (c >> 3)).astype(BF16)
        wide = dot(got, rep)
        tile = []
        for k in range(2):
            part = wide[k * BINS:(k + 1) * BINS]
            two = [(part[:, 128 * j:128 * j + 128] * diag).reshape(GROUPS, 8, 128) for j in range(2)]
            tile.append(cat(two, axis=1).astype(BF16))
        nodal[:, cp * 16:cp * 16 + 16, 0:128] = tile[0]
        nodal[:, cp * 16:cp * 16 + 16, 128:256] = tile[0]
        nodal[:, cp * 16:cp * 16 + 16, 256:384] = tile[1]
    slots = lax.broadcasted_iota(jnp.int32, (128, BINS), 0)
    occ = jnp.where(slots < fill[...], 1.0, 0.0).T
    state[0:3] = pos[...]
    state[3:6] = vel[...]
    state[6] = relax[...] * occ
    state[7] = occ
    acc[...] = jnp.zeros_like(acc)

    def first(g, slot):
        rows = pl.ds(pl.multiple_of(g * 8, 8), 8)
        l0, l1, l2 = (basis(state[i, rows, :]) for i in range(3))
        lh, ll = split_tiles([b * c for b in l1 for c in l2])
        for a in range(4):
            s_first[slot, a] = l0[a]
        s_basis[slot] = lh
        s_nodal[slot] = dot(nodal[g], cat([lh, ll, lh], axis=0))

    def second(g, slot):
        rows = pl.ds(pl.multiple_of(g * 8, 8), 8)
        x = [state[i, rows, :] for i in range(3)]
        v = [state[3 + i, rows, :] for i in range(3)]
        ro, oc = state[6, rows, :], state[7, rows, :]
        l0 = [s_first[slot, a] for a in range(4)]
        stride = oc * 0.05
        forces = []
        for c in range(3):
            t = [l0[a] * s_nodal[slot, (4 * c + a) * 8:(4 * c + a) * 8 + 8] for a in range(4)]
            dv = ro * (((t[0] + t[1]) + (t[2] + t[3])) - v[c])
            nv = v[c] + dv
            state[3 + c, rows, :] = nv
            state[c, rows, :] = jnp.clip(x[c] + stride * nv, -1.0, 1.0)
            forces += [dv * l0[a] for a in range(4)]
        fh = cat([p.astype(BF16) for p in pairs(forces)], axis=0)
        wa = cat([p.astype(BF16) for p in pairs([oc * (l * l) for l in l0])], axis=0)
        lt = s_basis[slot].T
        acc[g, 0:96] += dot(fh, lt)
        acc[g, 96:128] += dot(wa, lt * lt)

    blocks = GROUPS // unroll

    def run(stage, i, side):
        for j in range(unroll):
            stage(lax.rem(i, blocks) * unroll + j, side * unroll + j)

    run(first, 0, 0)

    def body(k, _):
        i = 2 * k
        run(first, i + 1, 1)
        run(second, i, 0)
        run(first, i + 2, 0)
        run(second, i + 1, 1)
        return 0

    n = SUBSTEPS * blocks
    lax.fori_loop(0, n // 2 - 1, body, 0)
    run(first, n - 1, 1)
    run(second, n - 2, 0)
    run(second, n - 1, 1)
    pout[...] = state[0:6]
    sums = jnp.zeros((2 * BINS, 256), F32)
    for cp in range(8):
        two = cat([acc[:, (2 * cp + j) * 8:(2 * cp + j) * 8 + 8, :].reshape(BINS, 128) * diag for j in range(2)], axis=1)
        rep = ones_where((256, 256), lambda r, c: c == cp * 32 + (r >> 3)).astype(BF16)
        sums += dot(cat(split(two), axis=0), rep)
    sums = cat(split((sums[:BINS] + sums[BINS:]).T), axis=1)
    lanes = lax.broadcasted_iota(jnp.int32, (BINS, 256), 1).astype(F32)
    for r in range(8):
        hot = jnp.where(column == lanes + float(r * 256), 1.0, 0.0).astype(BF16)
        dep = dot(sums, cat([hot, hot], axis=0))
        inv = 1.0 / (mass[r:r + 1, :] + dep[192:256])
        for c in range(3):
            change = dep[c * 64:c * 64 + 64] * inv
            for h in range(2):
                s = pl.ds(c * 1024 + 8 * h + r, 64, stride=16)
                coupled[s, :] = fluid[s, :] - change[:, 128 * h:128 * h + 128]


def cell(src, n, rows=slice(None)):
    if src.shape[0] == BINS:
        return src[n, rows]
    return cat([src[2 * n, rows], src[2 * n + 1, rows]], axis=1)


def half(src, n, base):
    return src[n, :, base:base + 128] if src.shape[0] == BINS else src[2 * n + base // 128]


def curvature(line):
    low = line[0] - 2.0 * line[1] + line[2]
    high = line[1] - 2.0 * line[2] + line[3]
    step = low - high
    return [low + step, low, high, high - step]


CURVE = ((-2, 3, -1), (-1, 1, 0), (0, -1, 1), (1, -3, 2))
SLOPE = ((11, -7, 2), (2, 5, -1), (-1, 5, 2), (2, -7, 11))


def section_phase(src, dst, visc, sub, comp):
    up = jnp.where(sub == 7, 0.0, 0.25)
    down = jnp.where(sub == 0, 0.0, 0.25)

    def body(i, _):
        base = comp * 64 + i * 16
        t = [[cell(src, base + 4 * b + c) for c in range(4)] for b in range(4)]
        across = [curvature([t[b][c] for b in range(4)]) for c in range(4)]
        for b in range(4):
            along = curvature(t[b])
            for c in range(4):
                new = t[b][c] + visc * (along[c] + across[c][b])
                if b == 3:
                    new = new - 0.25 * t[3][c] + up * pltpu.roll(t[0][c], 7, 0)
                if b == 0:
                    new = new - 0.25 * t[0][c] + down * pltpu.roll(t[3][c], 1, 0)
                dst[base + 4 * b + c] = new
        return 0

    lax.fori_loop(0, 4, body, 0, unroll=2)


def airway_phase(src, dst, mix, lane, comp):
    fore = jnp.where(lane == 255, 0.0, 0.25)
    back = jnp.where(lane == 0, 0.0, 0.25)

    def body(i, _):
        base = comp * 64 + i * 4
        for c in range(4):
            at = [base + 16 * a + c for a in range(4)]
            q = [cell(src, n) for n in at]
            d = [q[k + 1] - q[k] for k in range(3)]
            for a in range(4):
                new = dst[at[a]] + mix[3 * a] * d[0] + mix[3 * a + 1] * d[1] + mix[3 * a + 2] * d[2]
                if a == 3:
                    new = new - 0.25 * q[3] + fore * pltpu.roll(q[0], 255, 1)
                if a == 0:
                    new = new - 0.25 * q[0] + back * pltpu.roll(q[3], 1, 1)
                dst[at[a]] = new
        return 0

    lax.fori_loop(0, 4, body, 0, unroll=2)


def air_nodes(a, comp):
    return [comp * 64 + a * 16 + k for k in range(16)]


def sec_nodes(b, comp):
    return [comp * 64 + a * 16 + b * 4 + c for a in range(4) for c in range(4)]


def kernel(unroll, elem, fill, fluid, mass, pos, vel, relax, viscosity, speed, out, pout, nodal, state, acc, s_basis,
           s_nodal, s_first, field, ping, pong, mix, s_sec, s_air, r_sec, r_air, s_cor, r_cor, send_sem, recv_sem):
    me_a, me_s = lax.axis_index("airway"), lax.axis_index("section")
    n_a, n_s = lax.axis_size("airway"), lax.axis_size("section")
    peers = [(me_a, lax.rem(me_s + 1, n_s)), (me_a, lax.rem(me_s + n_s - 1, n_s)),
             (lax.rem(me_a + 1, n_a), me_s), (lax.rem(me_a + n_a - 1, n_a), me_s)]
    peers += [(peers[2 + a][0], peers[b][1]) for b in range(2) for a in range(2)]
    barrier = pltpu.get_barrier_semaphore()
    for p in peers:
        pl.semaphore_signal(barrier, inc=1, device_id=p, device_id_type=MESH)
    drag_part(unroll, elem, fill, fluid, mass, pos, vel, relax, field.reshape(3072, 128), pout, nodal, state, acc, s_basis,
              s_nodal, s_first)
    visc = viscosity[...] * 2.25
    quarter = speed[...] * 0.25
    for a in range(4):
        for k in range(3):
            mix[3 * a + k] = CURVE[a][k] * visc - SLOPE[a][k] * quarter
    sub = lax.broadcasted_iota(jnp.int32, (8, 256), 0)
    lane = lax.broadcasted_iota(jnp.int32, (8, 256), 1)
    lane1 = lax.broadcasted_iota(jnp.int32, (8, 128), 1)
    sub1 = lax.broadcasted_iota(jnp.int32, (8, 128), 0)
    some = lambda cond: jnp.where(cond, 0.25, 0.0).astype(F32)
    next_s, prev_s = some(me_s < n_s - 1), some(me_s > 0)
    next_a, prev_a = some(me_a < n_a - 1), some(me_a > 0)
    pl.semaphore_wait(barrier, 8)
    bufs = [field, ping, pong, ping, out]
    flying = {}

    def send(p, comp):
        src = bufs[p]
        for slot, row, b in ((0, 7, 3), (1, 0, 0)):
            for j, n in enumerate(sec_nodes(b, comp)):
                s_sec[p, comp, slot, j:j + 1, :] = cell(src, n, slice(row, row + 1))
        copies = [start(p, comp, k, s_sec.at[p, comp, k], r_sec.at[p, comp, k]) for k in range(2)]
        for slot, base, a in ((0, 128, 3), (1, 0, 0)):
            packed = jnp.zeros((8, 128), F32)
            col = 127 if slot == 0 else 0
            for j, n in enumerate(air_nodes(a, comp)):
                moved = pltpu.roll(half(src, n, base), (j - col) % 128, 1)
                packed = jnp.where(lane1 == j, moved, packed)
            s_air[p, comp, slot] = packed
        copies += [start(p, comp, 2 + k, s_air.at[p, comp, k], r_air.at[p, comp, k]) for k in range(2)]
        if p % 2 == 0:
            for b in range(2):
                for a in range(2):
                    rows = s_sec[p, comp, b, 12 - 12 * a:16 - 12 * a, (1 - a) * 128:(2 - a) * 128]
                    rows = pltpu.roll(cat([rows, rows], axis=0), 1 if a == 0 else 127, 1)
                    s_cor[p // 2, comp, 2 * b + a, 0] = jnp.where(lane1 == 127 * a, rows, 0.0)
                    tile = pltpu.roll(s_air[p, comp, a], 1 if b == 0 else 7, 0)
                    tile = pltpu.roll(tile, 116 if b == 0 else 12, 1)
                    hit = (sub1 == 7 * b) & (lane1 // 4 == 3 * b)
                    s_cor[p // 2, comp, 2 * b + a, 1] = jnp.where(hit, tile, 0.0)
                    k = 2 * b + a
                    copies.append(start(p, comp, 4 + k, s_cor.at[p // 2, comp, k], r_cor.at[p // 2, comp, k]))
        flying[p, comp] = copies

    def start(p, comp, k, s, r):
        copy = pltpu.make_async_remote_copy(
            src_ref=s, dst_ref=r, send_sem=send_sem.at[p, comp, k], recv_sem=recv_sem.at[p, comp, k],
            device_id=peers[k], device_id_type=MESH)
        copy.start()
        return copy

    def complete(p, comp):
        for c in flying[p + 1, comp]:
            c.wait()
        for c in flying[p, comp][4:]:
            c.wait()
        near = [[r_cor[p // 2, comp, 2 * b + a] for a in range(2)] for b in range(2)]
        for slot in range(2):
            r_sec[p + 1, comp, slot] += 0.25 * s_sec[p, comp, 1 - slot]
            r_air[p + 1, comp, slot] += 0.25 * s_air[p, comp, 1 - slot]
            for other in range(2):
                scale = (prev_a, next_a)[other]
                low = 12 * other
                r_sec[p + 1, comp, slot, low:low + 4, other * 128:other * 128 + 128] += scale * near[slot][other][0, 0:4]
                scale = (prev_s, next_s)[other]
                r_air[p + 1, comp, slot] += scale * near[other][slot][1]

    def receive(p, comp):
        dst = bufs[p + 1]
        if p % 2 == 0:
            for c in flying[p, comp][:4]:
                c.wait()
        else:
            complete(p - 1, comp)
        for slot, row, b, scale in ((0, 0, 0, prev_s), (1, 7, 3, next_s)):
            for j, n in enumerate(sec_nodes(b, comp)):
                dst[n, row:row + 1, :] += scale * r_sec[p, comp, slot, j:j + 1, :]
        for slot, base, a, scale in ((0, 0, 0, prev_a), (1, 128, 3, next_a)):
            col = 0 if slot == 0 else 127
            packed = r_air[p, comp, slot] * scale
            for j, n in enumerate(air_nodes(a, comp)):
                moved = pltpu.roll(packed, (col - j) % 128, 1)
                dst[n, :, base:base + 128] += jnp.where(lane1 == col, moved, 0.0)

    def advance_one(p, comp):
        section_phase(bufs[p], bufs[p + 1], visc, sub, comp)
        airway_phase(bufs[p], bufs[p + 1], mix, lane, comp)

    for p in range(0, PASSES, 2):
        for comp in range(3):
            if p:
                receive(p - 1, comp)
            send(p, comp)
            advance_one(p, comp)
            send(p + 1, comp)
        for comp in range(3):
            receive(p, comp)
            advance_one(p + 1, comp)
    for comp in range(3):
        receive(PASSES - 1, comp)


def local(fluid_velocity, viscosity, axial_speed, fluid_mass, positions, velocities, relax_rates, bin_element, bin_fill):
    unroll = 12
    fluid = fluid_velocity.reshape(192, 8, 2, 128).transpose(0, 2, 1, 3).reshape(3072, 128)
    vm = pl.BlockSpec(memory_space=pltpu.VMEM)
    faces = pltpu.VMEM((PASSES, 3, 2, 16, 256), F32)
    edges = pltpu.VMEM((PASSES, 3, 2, 8, 128), F32)
    corners = pltpu.VMEM((PASSES // 2, 3, 4, 2, 8, 128), F32)
    field = pltpu.VMEM((192, 8, 256), F32)
    done, moved = pl.pallas_call(
        functools.partial(kernel, unroll),
        out_shape=(pltpu.VMEM((192, 8, 256), F32), pltpu.VMEM((6, BINS, 128), F32)),
        in_specs=[vm] * 9,
        out_specs=(vm, vm),
        scratch_shapes=[pltpu.VMEM((GROUPS, 96, 384), BF16), pltpu.VMEM((8, BINS, 128), F32),
                        pltpu.VMEM((GROUPS, 128, 128), F32), pltpu.VMEM((2 * unroll, 128, 128), BF16),
                        pltpu.VMEM((2 * unroll, 96, 128), F32), pltpu.VMEM((2 * unroll, 4, 8, 128), F32),
                        pltpu.VMEM((384, 8, 128), F32), field, field, pltpu.VMEM((12, 8, 256), F32),
                        faces, edges, faces, edges, corners, corners,
                        pltpu.SemaphoreType.DMA((PASSES, 3, 8)), pltpu.SemaphoreType.DMA((PASSES, 3, 8))],
        compiler_params=pltpu.CompilerParams(collective_id=0, has_side_effects=True, vmem_limit_bytes=52 * 2**20),
    )(bin_element.reshape(1, BINS), bin_fill.reshape(1, BINS), fluid, fluid_mass, positions.transpose(1, 0, 2),
      velocities.transpose(1, 0, 2), relax_rates, viscosity, axial_speed)
    return done.reshape(fluid_velocity.shape), moved.transpose(1, 0, 2)


def solution(mesh):
    bins = ("airway", "section")
    cells = P("section", "airway")
    return jax.shard_map(
        local,
        mesh=mesh,
        in_specs=(P(None, None, *cells), cells, cells, cells, P(bins, None, None), P(bins, None, None), P(bins, None),
                  P(bins), P(bins)),
        out_specs=(P(None, None, *cells), P(bins, None, None)),
        check_vma=False,
    )
```

```python
import functools
import jax, jax.numpy as jnp, numpy as np
from jax import lax
from jax.experimental import pallas as pl
from jax.experimental.pallas import tpu as pltpu
from jax.sharding import PartitionSpec as P

F32, BF16 = jnp.float32, jnp.bfloat16
BINS, GROUPS, SUBSTEPS = 192, 24, 16
PASSES = 4
MESH = pl.DeviceIdType.MESH
cat = jnp.concatenate


def dot(a, b):
    return jnp.dot(a, b, preferred_element_type=F32)


def split(x):
    hi = x.astype(BF16)
    return hi, (x - hi.astype(F32)).astype(BF16)


def basis(x):
    s = x * x
    outer = s * (9 / 16) - (1 / 16)
    inner = s * (27 / 16) - (27 / 16)
    ends, mids = outer * x, inner * x
    third = inner * (1 / 3)
    return [outer - ends, mids - third, -(mids + third), outer + ends]


def pairs(tiles):
    return [cat(tiles[i:i + 2], axis=0) for i in range(0, len(tiles), 2)]


def split_tiles(tiles):
    both = [split(p) for p in pairs(tiles)]
    return cat([b[0] for b in both], axis=0), cat([b[1] for b in both], axis=0)


def ones_where(shape, same):
    r = lax.broadcasted_iota(jnp.int32, shape, 0)
    c = lax.broadcasted_iota(jnp.int32, shape, 1)
    return jnp.where(same(r, c), 1.0, 0.0)


def drag_part(unroll, elem, fill, fluid, mass, pos, vel, relax, coupled, pout, nodal, state, acc, s_basis, s_nodal,
              s_first):
    diag = ones_where((BINS, 128), lambda r, c: r % 8 == c % 8)
    column = jnp.broadcast_to(elem[...].astype(F32), (128, BINS)).T
    column = cat([column, column], axis=1)
    got = jnp.zeros((2 * BINS, BINS), F32)
    cells = lax.broadcasted_iota(jnp.int32, (256, BINS), 0)
    for r in range(8):
        hot = jnp.where(cells + r * 256 == elem[...], 1.0, 0.0).astype(BF16)
        got += dot(cat(split(cat([fluid[pl.ds(8 * h + r, BINS, stride=16), :] for h in range(2)], axis=1)), axis=0), hot)
    got = cat([got[:BINS].T, got[BINS:].T], axis=0).astype(BF16)
    mask = diag.astype(BF16)
    for cp in range(6):
        rep = ones_where((BINS, 256), lambda r, c: r == cp * 32 + (c >> 3)).astype(BF16)
        wide = dot(got, rep)
        tile = []
        for k in range(2):
            part = wide[k * BINS:(k + 1) * BINS]
            two = [(part[:, 128 * j:128 * j + 128] * diag).reshape(GROUPS, 8, 128) for j in range(2)]
            tile.append(cat(two, axis=1).astype(BF16))
        nodal[:, cp * 16:cp * 16 + 16, 0:128] = tile[0]
        nodal[:, cp * 16:cp * 16 + 16, 128:256] = tile[0]
        nodal[:, cp * 16:cp * 16 + 16, 256:384] = tile[1]
    slots = lax.broadcasted_iota(jnp.int32, (128, BINS), 0)
    occ = jnp.where(slots < fill[...], 1.0, 0.0).T
    state[0:3] = pos[...]
    state[3:6] = vel[...]
    state[6] = relax[...] * occ
    state[7] = occ
    acc[...] = jnp.zeros_like(acc)

    def first(g, slot):
        rows = slice(g * 8, g * 8 + 8)
        l0, l1, l2 = (basis(state[i, rows, :]) for i in range(3))
        lh, ll = split_tiles([b * c for b in l1 for c in l2])
        for a in range(4):
            s_first[slot, a] = l0[a]
        s_basis[slot] = lh
        s_nodal[slot] = dot(nodal[g], cat([lh, ll, lh], axis=0))

    def second(g, slot):
        rows = slice(g * 8, g * 8 + 8)
        x = [state[i, rows, :] for i in range(3)]
        v = [state[3 + i, rows, :] for i in range(3)]
        ro, oc = state[6, rows, :], state[7, rows, :]
        l0 = [s_first[slot, a] for a in range(4)]
        stride = oc * 0.05
        forces = []
        for c in range(3):
            t = [l0[a] * s_nodal[slot, (4 * c + a) * 8:(4 * c + a) * 8 + 8] for a in range(4)]
            dv = ro * (((t[0] + t[1]) + (t[2] + t[3])) - v[c])
            nv = v[c] + dv
            state[3 + c, rows, :] = nv
            state[c, rows, :] = jnp.clip(x[c] + stride * nv, -1.0, 1.0)
            forces += [dv * l0[a] for a in range(4)]
        fh = cat([p.astype(BF16) for p in pairs(forces)], axis=0)
        wa = cat([p.astype(BF16) for p in pairs([oc * (l * l) for l in l0])], axis=0)
        lt = s_basis[slot].T
        acc[g, 0:96] += dot(fh, lt)
        acc[g, 96:128] += dot(wa, lt * lt)

    blocks = GROUPS // unroll

    def run(stage, i, side):
        for j in range(unroll):
            stage(side * unroll + j, side * unroll + j)

    run(first, 0, 0)

    def body(k, _):
        i = 2 * k
        run(first, i + 1, 1)
        run(second, i, 0)
        run(first, i + 2, 0)
        run(second, i + 1, 1)
        return 0

    n = SUBSTEPS * blocks
    lax.fori_loop(0, n // 2 - 1, body, 0)
    run(first, n - 1, 1)
    run(second, n - 2, 0)
    run(second, n - 1, 1)
    pout[...] = state[0:6]
    sums = jnp.zeros((2 * BINS, 256), F32)
    for cp in range(8):
        two = cat([acc[:, (2 * cp + j) * 8:(2 * cp + j) * 8 + 8, :].reshape(BINS, 128) * diag for j in range(2)], axis=1)
        rep = ones_where((256, 256), lambda r, c: c == cp * 32 + (r >> 3)).astype(BF16)
        sums += dot(cat(split(two), axis=0), rep)
    sums = cat(split((sums[:BINS] + sums[BINS:]).T), axis=1)
    lanes = lax.broadcasted_iota(jnp.int32, (BINS, 256), 1).astype(F32)
    for r in range(8):
        hot = jnp.where(column == lanes + float(r * 256), 1.0, 0.0).astype(BF16)
        dep = dot(sums, cat([hot, hot], axis=0))
        inv = 1.0 / (mass[r:r + 1, :] + dep[192:256])
        for c in range(3):
            change = dep[c * 64:c * 64 + 64] * inv
            for h in range(2):
                s = pl.ds(c * 1024 + 8 * h + r, 64, stride=16)
                coupled[s, :] = fluid[s, :] - change[:, 128 * h:128 * h + 128]


def cell(src, n, rows=slice(None)):
    if src.shape[0] == BINS:
        return src[n, rows]
    return cat([src[2 * n, rows], src[2 * n + 1, rows]], axis=1)


def half(src, n, base):
    return src[n, :, base:base + 128] if src.shape[0] == BINS else src[2 * n + base // 128]


def curvature(line):
    low = line[0] - 2.0 * line[1] + line[2]
    high = line[1] - 2.0 * line[2] + line[3]
    step = low - high
    return [low + step, low, high, high - step]


CURVE = ((-2, 3, -1), (-1, 1, 0), (0, -1, 1), (1, -3, 2))
SLOPE = ((11, -7, 2), (2, 5, -1), (-1, 5, 2), (2, -7, 11))


def section_phase(src, dst, visc, sub, comp):
    up = jnp.where(sub == 7, 0.0, 0.25)
    down = jnp.where(sub == 0, 0.0, 0.25)

    def body(i, _):
        base = comp * 64 + i * 16
        t = [[cell(src, base + 4 * b + c) for c in range(4)] for b in range(4)]
        across = [curvature([t[b][c] for b in range(4)]) for c in range(4)]
        for b in range(4):
            along = curvature(t[b])
            for c in range(4):
                new = t[b][c] + visc * (along[c] + across[c][b])
                if b == 3:
                    new = new - 0.25 * t[3][c] + up * pltpu.roll(t[0][c], 7, 0)
                if b == 0:
                    new = new - 0.25 * t[0][c] + down * pltpu.roll(t[3][c], 1, 0)
                dst[base + 4 * b + c] = new
        return 0

    lax.fori_loop(0, 4, body, 0, unroll=2)


def airway_phase(src, dst, mix, lane, comp):
    fore = jnp.where(lane == 255, 0.0, 0.25)
    back = jnp.where(lane == 0, 0.0, 0.25)

    def body(i, _):
        base = comp * 64 + i * 4
        for c in range(4):
            at = [base + 16 * a + c for a in range(4)]
            q = [cell(src, n) for n in at]
            d = [q[k + 1] - q[k] for k in range(3)]
            for a in range(4):
                new = dst[at[a]] + mix[3 * a] * d[0] + mix[3 * a + 1] * d[1] + mix[3 * a + 2] * d[2]
                if a == 3:
                    new = new - 0.25 * q[3] + fore * pltpu.roll(q[0], 255, 1)
                if a == 0:
                    new = new - 0.25 * q[0] + back * pltpu.roll(q[3], 1, 1)
                dst[at[a]] = new
        return 0

    lax.fori_loop(0, 4, body, 0, unroll=2)


def air_nodes(a, comp):
    return [comp * 64 + a * 16 + k for k in range(16)]


def sec_nodes(b, comp):
    return [comp * 64 + a * 16 + b * 4 + c for a in range(4) for c in range(4)]


def kernel(unroll, elem, fill, fluid, mass, pos, vel, relax, viscosity, speed, out, pout, nodal, state, acc, s_basis,
           s_nodal, s_first, field, ping, pong, mix, s_sec, s_air, r_sec, r_air, s_cor, r_cor, send_sem, recv_sem):
    me_a, me_s = lax.axis_index("airway"), lax.axis_index("section")
    n_a, n_s = lax.axis_size("airway"), lax.axis_size("section")
    peers = [(me_a, lax.rem(me_s + 1, n_s)), (me_a, lax.rem(me_s + n_s - 1, n_s)),
             (lax.rem(me_a + 1, n_a), me_s), (lax.rem(me_a + n_a - 1, n_a), me_s)]
    peers += [(peers[2 + a][0], peers[b][1]) for b in range(2) for a in range(2)]
    barrier = pltpu.get_barrier_semaphore()
    for p in peers:
        pl.semaphore_signal(barrier, inc=1, device_id=p, device_id_type=MESH)
    drag_part(unroll, elem, fill, fluid, mass, pos, vel, relax, field.reshape(3072, 128), pout, nodal, state, acc, s_basis,
              s_nodal, s_first)
    visc = viscosity[...] * 2.25
    quarter = speed[...] * 0.25
    for a in range(4):
        for k in range(3):
            mix[3 * a + k] = CURVE[a][k] * visc - SLOPE[a][k] * quarter
    sub = lax.broadcasted_iota(jnp.int32, (8, 256), 0)
    lane = lax.broadcasted_iota(jnp.int32, (8, 256), 1)
    lane1 = lax.broadcasted_iota(jnp.int32, (8, 128), 1)
    sub1 = lax.broadcasted_iota(jnp.int32, (8, 128), 0)
    some = lambda cond: jnp.where(cond, 0.25, 0.0).astype(F32)
    next_s, prev_s = some(me_s < n_s - 1), some(me_s > 0)
    next_a, prev_a = some(me_a < n_a - 1), some(me_a > 0)
    pl.semaphore_wait(barrier, 8)
    bufs = [field, ping, pong, ping, out]
    flying = {}

    def send(p, comp):
        src = bufs[p]
        for slot, row, b in ((0, 7, 3), (1, 0, 0)):
            for j, n in enumerate(sec_nodes(b, comp)):
                s_sec[p, comp, slot, j:j + 1, :] = cell(src, n, slice(row, row + 1))
        copies = [start(p, comp, k, s_sec.at[p, comp, k], r_sec.at[p, comp, k]) for k in range(2)]
        for slot, base, a in ((0, 128, 3), (1, 0, 0)):
            packed = jnp.zeros((8, 128), F32)
            col = 127 if slot == 0 else 0
            for j, n in enumerate(air_nodes(a, comp)):
                moved = pltpu.roll(half(src, n, base), (j - col) % 128, 1)
                packed = jnp.where(lane1 == j, moved, packed)
            s_air[p, comp, slot] = packed
        copies += [start(p, comp, 2 + k, s_air.at[p, comp, k], r_air.at[p, comp, k]) for k in range(2)]
        if p % 2 == 0:
            for b in range(2):
                for a in range(2):
                    rows = s_sec[p, comp, b, 12 - 12 * a:16 - 12 * a, (1 - a) * 128:(2 - a) * 128]
                    rows = pltpu.roll(cat([rows, rows], axis=0), 1 if a == 0 else 127, 1)
                    s_cor[p // 2, comp, 2 * b + a, 0] = jnp.where(lane1 == 127 * a, rows, 0.0)
                    tile = pltpu.roll(s_air[p, comp, a], 1 if b == 0 else 7, 0)
                    tile = pltpu.roll(tile, 116 if b == 0 else 12, 1)
                    hit = (sub1 == 7 * b) & (lane1 // 4 == 3 * b)
                    s_cor[p // 2, comp, 2 * b + a, 1] = jnp.where(hit, tile, 0.0)
                    k = 2 * b + a
                    copies.append(start(p, comp, 4 + k, s_cor.at[p // 2, comp, k], r_cor.at[p // 2, comp, k]))
        flying[p, comp] = copies

    def start(p, comp, k, s, r):
        copy = pltpu.make_async_remote_copy(
            src_ref=s, dst_ref=r, send_sem=send_sem.at[p, comp, k], recv_sem=recv_sem.at[p, comp, k],
            device_id=peers[k], device_id_type=MESH)
        copy.start()
        return copy

    def complete(p, comp):
        for c in flying[p + 1, comp]:
            c.wait()
        for c in flying[p, comp][4:]:
            c.wait()
        near = [[r_cor[p // 2, comp, 2 * b + a] for a in range(2)] for b in range(2)]
        for slot in range(2):
            r_sec[p + 1, comp, slot] += 0.25 * s_sec[p, comp, 1 - slot]
            r_air[p + 1, comp, slot] += 0.25 * s_air[p, comp, 1 - slot]
            for other in range(2):
                scale = (prev_a, next_a)[other]
                low = 12 * other
                r_sec[p + 1, comp, slot, low:low + 4, other * 128:other * 128 + 128] += scale * near[slot][other][0, 0:4]
                scale = (prev_s, next_s)[other]
                r_air[p + 1, comp, slot] += scale * near[other][slot][1]

    def receive(p, comp):
        dst = bufs[p + 1]
        if p % 2 == 0:
            for c in flying[p, comp][:4]:
                c.wait()
        else:
            complete(p - 1, comp)
        for slot, row, b, scale in ((0, 0, 0, prev_s), (1, 7, 3, next_s)):
            for j, n in enumerate(sec_nodes(b, comp)):
                dst[n, row:row + 1, :] += scale * r_sec[p, comp, slot, j:j + 1, :]
        for slot, base, a, scale in ((0, 0, 0, prev_a), (1, 128, 3, next_a)):
            col = 0 if slot == 0 else 127
            packed = r_air[p, comp, slot] * scale
            for j, n in enumerate(air_nodes(a, comp)):
                moved = pltpu.roll(packed, (col - j) % 128, 1)
                dst[n, :, base:base + 128] += jnp.where(lane1 == col, moved, 0.0)

    def advance_one(p, comp):
        section_phase(bufs[p], bufs[p + 1], visc, sub, comp)
        airway_phase(bufs[p], bufs[p + 1], mix, lane, comp)

    for p in range(0, PASSES, 2):
        for comp in range(3):
            if p:
                receive(p - 1, comp)
            send(p, comp)
            advance_one(p, comp)
            send(p + 1, comp)
        for comp in range(3):
            receive(p, comp)
            advance_one(p + 1, comp)
    for comp in range(3):
        receive(PASSES - 1, comp)


def local(fluid_velocity, viscosity, axial_speed, fluid_mass, positions, velocities, relax_rates, bin_element, bin_fill):
    unroll = 12
    fluid = fluid_velocity.reshape(192, 8, 2, 128).transpose(0, 2, 1, 3).reshape(3072, 128)
    vm = pl.BlockSpec(memory_space=pltpu.VMEM)
    faces = pltpu.VMEM((PASSES, 3, 2, 16, 256), F32)
    edges = pltpu.VMEM((PASSES, 3, 2, 8, 128), F32)
    corners = pltpu.VMEM((PASSES // 2, 3, 4, 2, 8, 128), F32)
    field = pltpu.VMEM((192, 8, 256), F32)
    done, moved = pl.pallas_call(
        functools.partial(kernel, unroll),
        out_shape=(pltpu.VMEM((192, 8, 256), F32), pltpu.VMEM((6, BINS, 128), F32)),
        in_specs=[vm] * 9,
        out_specs=(vm, vm),
        scratch_shapes=[pltpu.VMEM((GROUPS, 96, 384), BF16), pltpu.VMEM((8, BINS, 128), F32),
                        pltpu.VMEM((GROUPS, 128, 128), F32), pltpu.VMEM((2 * unroll, 128, 128), BF16),
                        pltpu.VMEM((2 * unroll, 96, 128), F32), pltpu.VMEM((2 * unroll, 4, 8, 128), F32),
                        pltpu.VMEM((384, 8, 128), F32), field, field, pltpu.VMEM((12, 8, 256), F32),
                        faces, edges, faces, edges, corners, corners,
                        pltpu.SemaphoreType.DMA((PASSES, 3, 8)), pltpu.SemaphoreType.DMA((PASSES, 3, 8))],
        compiler_params=pltpu.CompilerParams(collective_id=0, has_side_effects=True, vmem_limit_bytes=52 * 2**20),
    )(bin_element.reshape(1, BINS), bin_fill.reshape(1, BINS), fluid, fluid_mass, positions.transpose(1, 0, 2),
      velocities.transpose(1, 0, 2), relax_rates, viscosity, axial_speed)
    return done.reshape(fluid_velocity.shape), moved.transpose(1, 0, 2)


def solution(mesh):
    bins = ("airway", "section")
    cells = P("section", "airway")
    return jax.shard_map(
        local,
        mesh=mesh,
        in_specs=(P(None, None, *cells), cells, cells, cells, P(bins, None, None), P(bins, None, None), P(bins, None),
                  P(bins), P(bins)),
        out_specs=(P(None, None, *cells), P(bins, None, None)),
        check_vma=False,
    )
```

```python
import functools
import jax, jax.numpy as jnp, numpy as np
from jax import lax
from jax.experimental import pallas as pl
from jax.experimental.pallas import tpu as pltpu
from jax.sharding import PartitionSpec as P

F32, BF16 = jnp.float32, jnp.bfloat16
BINS, GROUPS, SUBSTEPS = 192, 24, 16
PASSES = 4
MESH = pl.DeviceIdType.MESH
cat = jnp.concatenate


def dot(a, b):
    return jnp.dot(a, b, preferred_element_type=F32)


def split(x):
    hi = x.astype(BF16)
    return hi, (x - hi.astype(F32)).astype(BF16)


def basis(x):
    s = x * x
    outer, inner = s - 1 / 9, s - 1.0
    ends, mids, third = outer * x, inner * x, inner * (1 / 3)
    return [outer - ends, mids - third, mids + third, outer + ends]


def node_scale(shape, axis):
    n = lax.broadcasted_iota(jnp.int32, shape, axis)
    scale = jnp.ones(shape, F32)
    for shift in (4, 2, 0):
        k = (n >> shift) & 3
        scale = scale * jnp.where(k == 1, 27 / 16, jnp.where(k == 2, -27 / 16, 9 / 16))
    return scale


def pairs(tiles):
    return [cat(tiles[i:i + 2], axis=0) for i in range(0, len(tiles), 2)]


def split_tiles(tiles):
    both = [split(p) for p in pairs(tiles)]
    return cat([b[0] for b in both], axis=0), cat([b[1] for b in both], axis=0)


def ones_where(shape, same):
    r = lax.broadcasted_iota(jnp.int32, shape, 0)
    c = lax.broadcasted_iota(jnp.int32, shape, 1)
    return jnp.where(same(r, c), 1.0, 0.0)


def drag_part(unroll, elem, fill, fluid, mass, pos, vel, relax, coupled, pout, nodal, state, acc, s_basis, s_nodal,
              s_first):
    diag = ones_where((BINS, 128), lambda r, c: r % 8 == c % 8)
    column = jnp.broadcast_to(elem[...].astype(F32), (128, BINS)).T
    column = cat([column, column], axis=1)
    got = jnp.zeros((2 * BINS, BINS), F32)
    cells = lax.broadcasted_iota(jnp.int32, (256, BINS), 0)
    for r in range(8):
        hot = jnp.where(cells + r * 256 == elem[...], 1.0, 0.0).astype(BF16)
        got += dot(cat(split(cat([fluid[pl.ds(8 * h + r, BINS, stride=16), :] for h in range(2)], axis=1)), axis=0), hot)
    got = cat(split((got[:BINS].T + got[BINS:].T) * node_scale((BINS, BINS), 1)), axis=0)
    mask = diag.astype(BF16)
    for cp in range(6):
        rep = ones_where((BINS, 256), lambda r, c: r == cp * 32 + (c >> 3)).astype(BF16)
        wide = dot(got, rep)
        tile = []
        for k in range(2):
            part = wide[k * BINS:(k + 1) * BINS]
            two = [(part[:, 128 * j:128 * j + 128] * diag).reshape(GROUPS, 8, 128) for j in range(2)]
            tile.append(cat(two, axis=1).astype(BF16))
        nodal[:, cp * 16:cp * 16 + 16, 0:128] = tile[0]
        nodal[:, cp * 16:cp * 16 + 16, 128:256] = tile[0]
        nodal[:, cp * 16:cp * 16 + 16, 256:384] = tile[1]
    slots = lax.broadcasted_iota(jnp.int32, (128, BINS), 0)
    occ = jnp.where(slots < fill[...], 1.0, 0.0).T
    state[0:3] = pos[...]
    state[3:6] = vel[...]
    state[6] = relax[...] * occ
    state[7] = occ
    acc[...] = jnp.zeros_like(acc)

    def first(g, slot):
        rows = slice(g * 8, g * 8 + 8)
        l0, l1, l2 = (basis(state[i, rows, :]) for i in range(3))
        lh, ll = split_tiles([b * c for b in l1 for c in l2])
        for a in range(4):
            s_first[slot, a] = l0[a]
        s_basis[slot] = lh
        s_nodal[slot] = dot(nodal[g], cat([lh, ll, lh], axis=0))

    def second(g, slot):
        rows = slice(g * 8, g * 8 + 8)
        x = [state[i, rows, :] for i in range(3)]
        v = [state[3 + i, rows, :] for i in range(3)]
        ro, oc = state[6, rows, :], state[7, rows, :]
        l0 = [s_first[slot, a] for a in range(4)]
        stride = oc * 0.05
        forces = []
        for c in range(3):
            t = [l0[a] * s_nodal[slot, (4 * c + a) * 8:(4 * c + a) * 8 + 8] for a in range(4)]
            dv = ro * (((t[0] + t[1]) + (t[2] + t[3])) - v[c])
            nv = v[c] + dv
            state[3 + c, rows, :] = nv
            state[c, rows, :] = jnp.clip(x[c] + stride * nv, -1.0, 1.0)
            forces += [dv * l0[a] for a in range(4)]
        fh = cat([p.astype(BF16) for p in pairs(forces)], axis=0)
        wa = cat([p.astype(BF16) for p in pairs([oc * (l * l) for l in l0])], axis=0)
        lt = s_basis[slot].T
        acc[g, 0:96] += dot(fh, lt)
        acc[g, 96:128] += dot(wa, lt * lt)

    blocks = GROUPS // unroll

    def run(stage, i, side):
        for j in range(unroll):
            stage(side * unroll + j, side * unroll + j)

    run(first, 0, 0)

    def body(k, _):
        i = 2 * k
        run(first, i + 1, 1)
        run(second, i, 0)
        run(first, i + 2, 0)
        run(second, i + 1, 1)
        return 0

    n = SUBSTEPS * blocks
    lax.fori_loop(0, n // 2 - 1, body, 0)
    run(first, n - 1, 1)
    run(second, n - 2, 0)
    run(second, n - 1, 1)
    pout[...] = state[0:6]
    sums = jnp.zeros((2 * BINS, 256), F32)
    for cp in range(8):
        two = cat([acc[:, (2 * cp + j) * 8:(2 * cp + j) * 8 + 8, :].reshape(BINS, 128) * diag for j in range(2)], axis=1)
        rep = ones_where((256, 256), lambda r, c: c == cp * 32 + (r >> 3)).astype(BF16)
        sums += dot(cat(split(two), axis=0), rep)
    scale = node_scale((256, BINS), 0)
    scale = cat([scale[:BINS], scale[BINS:] * scale[BINS:]], axis=0)
    sums = cat(split((sums[:BINS] + sums[BINS:]).T * scale), axis=1)
    lanes = lax.broadcasted_iota(jnp.int32, (BINS, 256), 1).astype(F32)
    for r in range(8):
        hot = jnp.where(column == lanes + float(r * 256), 1.0, 0.0).astype(BF16)
        dep = dot(sums, cat([hot, hot], axis=0))
        inv = 1.0 / (mass[r:r + 1, :] + dep[192:256])
        for c in range(3):
            change = dep[c * 64:c * 64 + 64] * inv
            for h in range(2):
                s = pl.ds(c * 1024 + 8 * h + r, 64, stride=16)
                coupled[s, :] = fluid[s, :] - change[:, 128 * h:128 * h + 128]


def cell(src, n, rows=slice(None)):
    if src.shape[0] == BINS:
        return src[n, rows]
    return cat([src[2 * n, rows], src[2 * n + 1, rows]], axis=1)


def half(src, n, base):
    return src[n, :, base:base + 128] if src.shape[0] == BINS else src[2 * n + base // 128]


def curvature(line):
    low = line[0] - 2.0 * line[1] + line[2]
    high = line[1] - 2.0 * line[2] + line[3]
    step = low - high
    return [low + step, low, high, high - step]


CURVE = ((-2, 3, -1), (-1, 1, 0), (0, -1, 1), (1, -3, 2))
SLOPE = ((11, -7, 2), (2, 5, -1), (-1, 5, 2), (2, -7, 11))


def section_phase(src, dst, visc, sub, comp):
    up = jnp.where(sub == 7, 0.0, 0.25)
    down = jnp.where(sub == 0, 0.0, 0.25)

    def body(i, _):
        base = comp * 64 + i * 16
        t = [[cell(src, base + 4 * b + c) for c in range(4)] for b in range(4)]
        across = [curvature([t[b][c] for b in range(4)]) for c in range(4)]
        for b in range(4):
            along = curvature(t[b])
            for c in range(4):
                new = t[b][c] + visc * (along[c] + across[c][b])
                if b == 3:
                    new = new - 0.25 * t[3][c] + up * pltpu.roll(t[0][c], 7, 0)
                if b == 0:
                    new = new - 0.25 * t[0][c] + down * pltpu.roll(t[3][c], 1, 0)
                dst[base + 4 * b + c] = new
        return 0

    lax.fori_loop(0, 4, body, 0, unroll=2)


def airway_phase(src, dst, mix, lane, comp):
    fore = jnp.where(lane == 255, 0.0, 0.25)
    back = jnp.where(lane == 0, 0.0, 0.25)

    def body(i, _):
        base = comp * 64 + i * 4
        for c in range(4):
            at = [base + 16 * a + c for a in range(4)]
            q = [cell(src, n) for n in at]
            d = [q[k + 1] - q[k] for k in range(3)]
            for a in range(4):
                new = dst[at[a]] + mix[3 * a] * d[0] + mix[3 * a + 1] * d[1] + mix[3 * a + 2] * d[2]
                if a == 3:
                    new = new - 0.25 * q[3] + fore * pltpu.roll(q[0], 255, 1)
                if a == 0:
                    new = new - 0.25 * q[0] + back * pltpu.roll(q[3], 1, 1)
                dst[at[a]] = new
        return 0

    lax.fori_loop(0, 4, body, 0, unroll=2)


def air_nodes(a, comp):
    return [comp * 64 + a * 16 + k for k in range(16)]


def sec_nodes(b, comp):
    return [comp * 64 + a * 16 + b * 4 + c for a in range(4) for c in range(4)]


def kernel(unroll, elem, fill, fluid, mass, pos, vel, relax, viscosity, speed, out, pout, nodal, state, acc, s_basis,
           s_nodal, s_first, field, ping, pong, mix, s_sec, s_air, r_sec, r_air, s_cor, r_cor, send_sem, recv_sem):
    me_a, me_s = lax.axis_index("airway"), lax.axis_index("section")
    n_a, n_s = lax.axis_size("airway"), lax.axis_size("section")
    peers = [(me_a, lax.rem(me_s + 1, n_s)), (me_a, lax.rem(me_s + n_s - 1, n_s)),
             (lax.rem(me_a + 1, n_a), me_s), (lax.rem(me_a + n_a - 1, n_a), me_s)]
    peers += [(peers[2 + a][0], peers[b][1]) for b in range(2) for a in range(2)]
    barrier = pltpu.get_barrier_semaphore()
    for p in peers:
        pl.semaphore_signal(barrier, inc=1, device_id=p, device_id_type=MESH)
    drag_part(unroll, elem, fill, fluid, mass, pos, vel, relax, field.reshape(3072, 128), pout, nodal, state, acc, s_basis,
              s_nodal, s_first)
    visc = viscosity[...] * 2.25
    quarter = speed[...] * 0.25
    for a in range(4):
        for k in range(3):
            mix[3 * a + k] = CURVE[a][k] * visc - SLOPE[a][k] * quarter
    sub = lax.broadcasted_iota(jnp.int32, (8, 256), 0)
    lane = lax.broadcasted_iota(jnp.int32, (8, 256), 1)
    lane1 = lax.broadcasted_iota(jnp.int32, (8, 128), 1)
    sub1 = lax.broadcasted_iota(jnp.int32, (8, 128), 0)
    some = lambda cond: jnp.where(cond, 0.25, 0.0).astype(F32)
    next_s, prev_s = some(me_s < n_s - 1), some(me_s > 0)
    next_a, prev_a = some(me_a < n_a - 1), some(me_a > 0)
    pl.semaphore_wait(barrier, 8)
    bufs = [field, ping, pong, ping, out]
    flying = {}

    def send(p, comp):
        src = bufs[p]
        for slot, row, b in ((0, 7, 3), (1, 0, 0)):
            for j, n in enumerate(sec_nodes(b, comp)):
                s_sec[p, comp, slot, j:j + 1, :] = cell(src, n, slice(row, row + 1))
        copies = [start(p, comp, k, s_sec.at[p, comp, k], r_sec.at[p, comp, k]) for k in range(2)]
        for slot, base, a in ((0, 128, 3), (1, 0, 0)):
            packed = jnp.zeros((8, 128), F32)
            col = 127 if slot == 0 else 0
            for j, n in enumerate(air_nodes(a, comp)):
                moved = pltpu.roll(half(src, n, base), (j - col) % 128, 1)
                packed = jnp.where(lane1 == j, moved, packed)
            s_air[p, comp, slot] = packed
        copies += [start(p, comp, 2 + k, s_air.at[p, comp, k], r_air.at[p, comp, k]) for k in range(2)]
        if p % 2 == 0:
            for b in range(2):
                for a in range(2):
                    rows = s_sec[p, comp, b, 12 - 12 * a:16 - 12 * a, (1 - a) * 128:(2 - a) * 128]
                    rows = pltpu.roll(cat([rows, rows], axis=0), 1 if a == 0 else 127, 1)
                    s_cor[p // 2, comp, 2 * b + a, 0] = jnp.where(lane1 == 127 * a, rows, 0.0)
                    tile = pltpu.roll(s_air[p, comp, a], 1 if b == 0 else 7, 0)
                    tile = pltpu.roll(tile, 116 if b == 0 else 12, 1)
                    hit = (sub1 == 7 * b) & (lane1 // 4 == 3 * b)
                    s_cor[p // 2, comp, 2 * b + a, 1] = jnp.where(hit, tile, 0.0)
                    k = 2 * b + a
                    copies.append(start(p, comp, 4 + k, s_cor.at[p // 2, comp, k], r_cor.at[p // 2, comp, k]))
        flying[p, comp] = copies

    def start(p, comp, k, s, r):
        copy = pltpu.make_async_remote_copy(
            src_ref=s, dst_ref=r, send_sem=send_sem.at[p, comp, k], recv_sem=recv_sem.at[p, comp, k],
            device_id=peers[k], device_id_type=MESH)
        copy.start()
        return copy

    def complete(p, comp):
        for c in flying[p + 1, comp]:
            c.wait()
        for c in flying[p, comp][4:]:
            c.wait()
        near = [[r_cor[p // 2, comp, 2 * b + a] for a in range(2)] for b in range(2)]
        for slot in range(2):
            r_sec[p + 1, comp, slot] += 0.25 * s_sec[p, comp, 1 - slot]
            r_air[p + 1, comp, slot] += 0.25 * s_air[p, comp, 1 - slot]
            for other in range(2):
                scale = (prev_a, next_a)[other]
                low = 12 * other
                r_sec[p + 1, comp, slot, low:low + 4, other * 128:other * 128 + 128] += scale * near[slot][other][0, 0:4]
                scale = (prev_s, next_s)[other]
                r_air[p + 1, comp, slot] += scale * near[other][slot][1]

    def receive(p, comp):
        dst = bufs[p + 1]
        if p % 2 == 0:
            for c in flying[p, comp][:4]:
                c.wait()
        else:
            complete(p - 1, comp)
        for slot, row, b, scale in ((0, 0, 0, prev_s), (1, 7, 3, next_s)):
            for j, n in enumerate(sec_nodes(b, comp)):
                dst[n, row:row + 1, :] += scale * r_sec[p, comp, slot, j:j + 1, :]
        for slot, base, a, scale in ((0, 0, 0, prev_a), (1, 128, 3, next_a)):
            col = 0 if slot == 0 else 127
            packed = r_air[p, comp, slot] * scale
            for j, n in enumerate(air_nodes(a, comp)):
                moved = pltpu.roll(packed, (col - j) % 128, 1)
                dst[n, :, base:base + 128] += jnp.where(lane1 == col, moved, 0.0)

    def advance_one(p, comp):
        section_phase(bufs[p], bufs[p + 1], visc, sub, comp)
        airway_phase(bufs[p], bufs[p + 1], mix, lane, comp)

    for p in range(0, PASSES, 2):
        for comp in range(3):
            if p:
                receive(p - 1, comp)
            send(p, comp)
            advance_one(p, comp)
            send(p + 1, comp)
        for comp in range(3):
            receive(p, comp)
            advance_one(p + 1, comp)
    for comp in range(3):
        receive(PASSES - 1, comp)


def local(fluid_velocity, viscosity, axial_speed, fluid_mass, positions, velocities, relax_rates, bin_element, bin_fill):
    unroll = 12
    fluid = fluid_velocity.reshape(192, 8, 2, 128).transpose(0, 2, 1, 3).reshape(3072, 128)
    vm = pl.BlockSpec(memory_space=pltpu.VMEM)
    faces = pltpu.VMEM((PASSES, 3, 2, 16, 256), F32)
    edges = pltpu.VMEM((PASSES, 3, 2, 8, 128), F32)
    corners = pltpu.VMEM((PASSES // 2, 3, 4, 2, 8, 128), F32)
    field = pltpu.VMEM((192, 8, 256), F32)
    done, moved = pl.pallas_call(
        functools.partial(kernel, unroll),
        out_shape=(pltpu.VMEM((192, 8, 256), F32), pltpu.VMEM((6, BINS, 128), F32)),
        in_specs=[vm] * 9,
        out_specs=(vm, vm),
        scratch_shapes=[pltpu.VMEM((GROUPS, 96, 384), BF16), pltpu.VMEM((8, BINS, 128), F32),
                        pltpu.VMEM((GROUPS, 128, 128), F32), pltpu.VMEM((2 * unroll, 128, 128), BF16),
                        pltpu.VMEM((2 * unroll, 96, 128), F32), pltpu.VMEM((2 * unroll, 4, 8, 128), F32),
                        pltpu.VMEM((384, 8, 128), F32), field, field, pltpu.VMEM((12, 8, 256), F32),
                        faces, edges, faces, edges, corners, corners,
                        pltpu.SemaphoreType.DMA((PASSES, 3, 8)), pltpu.SemaphoreType.DMA((PASSES, 3, 8))],
        compiler_params=pltpu.CompilerParams(collective_id=0, has_side_effects=True, vmem_limit_bytes=52 * 2**20),
    )(bin_element.reshape(1, BINS), bin_fill.reshape(1, BINS), fluid, fluid_mass, positions.transpose(1, 0, 2),
      velocities.transpose(1, 0, 2), relax_rates, viscosity, axial_speed)
    return done.reshape(fluid_velocity.shape), moved.transpose(1, 0, 2)


def solution(mesh):
    bins = ("airway", "section")
    cells = P("section", "airway")
    return jax.shard_map(
        local,
        mesh=mesh,
        in_specs=(P(None, None, *cells), cells, cells, cells, P(bins, None, None), P(bins, None, None), P(bins, None),
                  P(bins), P(bins)),
        out_specs=(P(None, None, *cells), P(bins, None, None)),
        check_vma=False,
    )
```
